256 devices in a mesh: col: 8 (over z), row: 32 (over y, x, core).
Axes of the slice: x: 4, y: 4, z: 8, core: 2. Of those that a mesh axis runs over, the one named last changes fastest.
Arguments:
- matrix: bfloat16 [24576, 24576], P('row', 'col'), may hold values from -9 to 9
- left_basis: float32 [320, 24576], P(None, ('row', 'col')), may hold values from -6 to 6
- right_basis: float32 [320, 24576], P(None, ('col', 'row')), may hold values from -6 to 6
- right_block: float32 [64, 24576], P(None, ('col', 'row')), may hold values from -6 to 6
Outputs:
- left_blocks: float32 [64, 24576], P(None, ('row', 'col'))
- right_blocks: float32 [64, 24576], P(None, ('col', 'row'))
- factors: float32 [2, 64, 64], replicated
The draws below stay inside these ranges and needn't reach their ends.
All inputs are finite; a program needn't handle non-finite values.
Results may differ from the reference program's by a relative error of at most 0.0041.
Values may be sent and summed in bfloat16 or wider, within the bound.
A program may use at most 64 MiB of HBM per device.

```python
import math
import jax
import jax.numpy as jnp
from jax import lax

N = 24576
BLOCK = 64
PRIOR = 5
STEPS = 1


def draw_matrix(key, part):
    first_key, second_key, third_key = jax.random.split(jax.random.fold_in(key, 17), 3)
    entries = jnp.clip(jax.random.normal(first_key, (N, N), jnp.float32), -6.0, 6.0)
    spread = math.log(4.0)
    ramp = 1.0 + 2.0 * jnp.arange(N, dtype=jnp.float32) / N
    row_scale = jnp.exp(jax.random.uniform(second_key, (N,), jnp.float32) * spread) * ramp
    col_scale = jnp.exp(jax.random.uniform(third_key, (N,), jnp.float32) * spread) * ramp
    scaled = entries * row_scale[:, None] * col_scale[None, :] / math.sqrt(N)
    scaled = jnp.clip(scaled, -9.0, 9.0)
    return scaled.astype(jnp.bfloat16)


def block_scale(own_key, extent, shards, smallest, largest):
    def one(dim, blocks):
        draws = jax.random.uniform(jax.random.fold_in(jax.random.fold_in(own_key, 6), dim), (blocks,), jnp.float32, smallest / len(shards), largest / len(shards))
        return jnp.repeat(jnp.exp(draws), extent[dim] // blocks).reshape((-1,) + (1,) * (len(extent) - dim - 1))

    level = one(*shards[0])
    for cut in shards[1:]:
        level = level * one(*cut)
    return level


def gaussian(own_key, extent, scale, most, shards=(), held_as=jnp.bfloat16):
    gain = block_scale(own_key, extent, shards, -0.22, 0.18) if shards else 1.0
    array = jax.random.normal(own_key, extent, jnp.float32) * scale * gain
    return jnp.minimum(jnp.maximum(array, -most), most).astype(held_as)


def setup_inputs(seed: int = 0) -> dict:
    arg_keys = jax.random.split(jax.random.key(seed), 5)
    return {
        "matrix": draw_matrix(jax.random.fold_in(arg_keys[4], 71), 0),
        "left_basis": gaussian(arg_keys[1], (PRIOR * BLOCK, N), 1.0, 6.0, ((1, 256),), jnp.float32),
        "right_basis": gaussian(arg_keys[2], (PRIOR * BLOCK, N), 1.0, 6.0, ((1, 256),), jnp.float32),
        "right_block": gaussian(arg_keys[3], (BLOCK, N), 1.0, 6.0, ((1, 256),), jnp.float32),
    }


highest_precision = lax.Precision.HIGHEST

def contract(first, second, contracted):
    return lax.dot_general(first, second, (contracted, ((), ())), precision=highest_precision)

def orthonormalize(image, basis_set):
    coefficients = contract(basis_set, image, ((1,), (1,))) / N
    projected = image - contract(coefficients, basis_set, ((0,), (0,)))
    gram_matrix = contract(projected, projected, ((1,), (1,))) / N
    factor_low = jnp.linalg.cholesky(gram_matrix)
    new_block = lax.linalg.triangular_solve(factor_low, projected, left_side=True, lower=True)
    return (new_block, factor_low)

def reference(matrix, left_basis, right_basis, right_block):
    left_set = left_basis
    right_set = jnp.concatenate([right_basis, right_block], 0)
    current = right_block
    left_found = []
    right_found = []
    factor_list = []
    for iteration in range(STEPS):
        image = lax.dot_general(current.astype(jnp.bfloat16).astype(jnp.float32), matrix.astype(jnp.float32), (((1,), (1,)), ((), ())), preferred_element_type=jnp.float32)
        left_new, left_low = orthonormalize(image, left_set)
        left_set = jnp.concatenate([left_set, left_new], 0)
        coimage = jnp.dot(left_new.astype(jnp.bfloat16).astype(jnp.float32), matrix.astype(jnp.float32), preferred_element_type=jnp.float32)
        right_new, right_low = orthonormalize(coimage, right_set)
        right_set = jnp.concatenate([right_set, right_new], 0)
        current = right_new
        left_found.append(left_new)
        right_found.append(right_new)
        factor_list.append(left_low)
        factor_list.append(right_low)
    return (jnp.concatenate(left_found, 0), jnp.concatenate(right_found, 0), jnp.stack(factor_list))
```

```python
import jax
import jax.numpy as jnp
from jax import lax
from jax.experimental import pallas as pl
from jax.experimental.pallas import tpu as pltpu
from jax.sharding import PartitionSpec as P

N = 24576
BLOCK = 64
PRIOR_ROWS = 320
SET_ROWS = 384
COLS = 8
ROWS = 32
WIDTH = 96
LANES = 128
MESH = pl.DeviceIdType.MESH
F32 = jnp.float32
BF16 = jnp.bfloat16
highest_precision = lax.Precision.HIGHEST


def dot_nn(first, second):
    return lax.dot_general(first, second, (((1,), (0,)), ((), ())), precision=highest_precision, preferred_element_type=F32)


def dot_nt(first, second):
    return lax.dot_general(first, second, (((1,), (1,)), ((), ())), precision=highest_precision, preferred_element_type=F32)


def wait_bytes(ref, sem):
    pltpu.make_async_copy(ref, ref, sem).wait()


def lanes_of(shape):
    return lax.broadcasted_iota(jnp.int32, shape, 1)


def cholesky_and_inverse(gram):
    lane = lanes_of((8, LANES))
    sub = lax.broadcasted_iota(jnp.int32, (8, LANES), 0)
    blocks = []
    for k in range(8):
        unit = jnp.where(lane == sub + (BLOCK + 8 * k), 1.0, 0.0)
        padded = jnp.concatenate([gram[8 * k : 8 * k + 8, :], jnp.zeros((8, BLOCK), F32)], axis=1)
        blocks.append(padded + unit)
    for j in range(BLOCK):
        own, s = j // 8, j % 8
        row = blocks[own][s : s + 1, :]
        inv = lax.rsqrt(row[:, j : j + 1])
        scaled = row * inv
        for k in range(own, 8):
            factor = blocks[k][:, j : j + 1] * inv
            updated = blocks[k] - factor * scaled
            if k == own:
                updated = jnp.where(sub > s, updated, jnp.where(sub == s, jnp.broadcast_to(scaled, (8, LANES)), blocks[k]))
            blocks[k] = updated
    return jnp.concatenate(blocks, axis=0)


def kernel(
    matrix_hbm, left_hbm, right_hbm, block_hbm,
    left_out, right_out, factors_out,
    matrix, left_in, right_in, block_in,
    left_set, right_set,
    b_slots, b_all, image_send, image_recv,
    u_slots, u_all, co_send, co_recv,
    p_local, p_rs, p_ar, p_all,
    g_local, g_rs, g_ar, g_all,
    load_sem, send_sem, b_sem, image_sem, u_sem, co_sem,
    p_rs_sem, p_ar_sem, p_ag_sem, g_rs_sem, g_ar_sem, g_ag_sem,
):
    col = lax.axis_index("col")
    row = lax.axis_index("row")
    q_left = lax.rem(col, 4)
    q_right = lax.rem(row, 4)

    def row_peer(o):
        return lax.rem(row + o, ROWS)

    def col_peer(o):
        return lax.rem(col + o, COLS)

    barrier = pltpu.get_barrier_semaphore()

    def greet_row(o, carry):
        pl.semaphore_signal(barrier, inc=1, device_id=(col, row_peer(o)), device_id_type=MESH)
        return carry

    def greet_col(o, carry):
        pl.semaphore_signal(barrier, inc=1, device_id=(col_peer(o), row), device_id_type=MESH)
        return carry

    load_block = pltpu.make_async_copy(block_hbm, block_in, load_sem.at[0])
    load_left = pltpu.make_async_copy(left_hbm, left_in, load_sem.at[1])
    load_right = pltpu.make_async_copy(right_hbm, right_in, load_sem.at[2])
    load_matrix = pltpu.make_async_copy(matrix_hbm, matrix, load_sem.at[3])
    load_block.start()
    lax.fori_loop(1, ROWS, greet_row, 0)
    lax.fori_loop(1, COLS, greet_col, 0)
    load_left.start()
    load_right.start()
    load_matrix.start()

    def send_row(source, target, sem, send):
        def body(o, carry):
            peer = row_peer(o)
            pltpu.make_async_remote_copy(
                src_ref=source(o, peer), dst_ref=target(o), send_sem=send, recv_sem=sem,
                device_id=(col, peer), device_id_type=MESH,
            ).start()
            return carry

        lax.fori_loop(1, ROWS, body, 0)

    def send_col(source, target, sem, send):
        def body(o, carry):
            peer = col_peer(o)
            pltpu.make_async_remote_copy(
                src_ref=source(o, peer), dst_ref=target(o), send_sem=send, recv_sem=sem,
                device_id=(peer, row), device_id_type=MESH,
            ).start()
            return carry

        lax.fori_loop(1, COLS, body, 0)

    right_shift = lax.rem(96 * q_right, LANES)
    left_shift = lax.rem(96 * q_left, LANES)
    right_back = lax.rem(32 * q_right, LANES)
    left_back = lax.rem(32 * q_left, LANES)

    right_set[...] = jnp.zeros_like(right_set)
    left_set[...] = jnp.zeros_like(left_set)
    load_block.wait()
    right_set[PRIOR_ROWS:SET_ROWS, 0:WIDTH] = block_in[...]
    turned_block = pltpu.roll(right_set[PRIOR_ROWS:SET_ROWS, :], right_shift, 1)
    right_set[PRIOR_ROWS:SET_ROWS, :] = turned_block
    b_slots[row] = turned_block.astype(BF16)
    pl.semaphore_wait(barrier, ROWS + COLS - 2)
    send_row(lambda o, peer: b_slots.at[row], lambda o: b_slots.at[row], b_sem, send_sem.at[0])

    load_left.wait()
    left_set[0:PRIOR_ROWS, 0:WIDTH] = left_in[...]
    left_set[0:PRIOR_ROWS, :] = pltpu.roll(left_set[0:PRIOR_ROWS, :], left_shift, 1)
    load_right.wait()
    right_set[0:PRIOR_ROWS, 0:WIDTH] = right_in[...]
    right_set[0:PRIOR_ROWS, :] = pltpu.roll(right_set[0:PRIOR_ROWS, :], right_shift, 1)

    def start_gram(side, basis):
        k = 0
        for i in range(3):
            for j in range(i + 1):
                block = dot_nt(basis[128 * i : 128 * i + 128, :], basis[128 * j : 128 * j + 128, :])
                g_local[side, 128 * k : 128 * k + 128, :] = block
                k += 1

    def gram_rs_send(side):
        send_row(lambda o, peer: g_local.at[side, pl.ds(pl.multiple_of(24 * peer, 8), 24)], lambda o: g_rs.at[side, o - 1], g_rs_sem.at[side], send_sem.at[1 + side])

    def gram_ar_send(side):
        wait_bytes(g_rs.at[side], g_rs_sem.at[side])
        total = g_local[side, pl.ds(pl.multiple_of(24 * row, 8), 24), :]
        for o in range(ROWS - 1):
            total = total + g_rs[side, o]
        g_ar[side, col] = total
        send_col(lambda o, peer: g_ar.at[side, col], lambda o: g_ar.at[side, col], g_ar_sem.at[side], send_sem.at[3 + side])

    def gram_ag_send(side):
        wait_bytes(g_ar.at[side, pl.ds(0, COLS - 1)], g_ar_sem.at[side])
        total = g_ar[side, 0]
        for c in range(1, COLS):
            total = total + g_ar[side, c]
        g_all[side, row] = total
        send_row(lambda o, peer: g_all.at[side, row], lambda o: g_all.at[side, row], g_ag_sem.at[side], send_sem.at[5 + side])

    def gram_wait(side):
        wait_bytes(g_all.at[side, pl.ds(0, ROWS - 1)], g_ag_sem.at[side])

    start_gram(0, left_set)

    lane16 = lanes_of((BLOCK, LANES))

    def joined(slots, out, count):
        for group in range(count // 4):
            first, second, third, fourth = (slots[4 * group + k].astype(F32) for k in range(4))
            base = 3 * LANES * group
            out[:, base : base + 128] = jnp.where(lane16 < 96, first, second).astype(BF16)
            out[:, base + 128 : base + 256] = jnp.where(lane16 < 64, second, third).astype(BF16)
            out[:, base + 256 : base + 384] = jnp.where(lane16 < 32, third, fourth).astype(BF16)

    def pieces(values):
        first, second, third = (values[:, 128 * k : 128 * k + 128] for k in range(3))
        return (first, jnp.where(lane16 < 64, second, first), jnp.where(lane16 < 64, third, second), third)

    wait_bytes(b_slots.at[pl.ds(0, ROWS - 1)], b_sem)
    gram_rs_send(0)
    joined(b_slots, b_all, ROWS)
    load_matrix.wait()
    for half in range(2):
        part = lax.dot_general(
            b_all[...], matrix[384 * half : 384 * half + 384, :], (((1,), (1,)), ((), ())), preferred_element_type=F32
        )
        for k, piece in enumerate(pieces(part)):
            image_send[4 * half + k] = piece
    send_col(lambda o, peer: image_send.at[peer], lambda o: image_recv.at[o - 1], image_sem, send_sem.at[7])
    start_gram(1, right_set)
    wait_bytes(image_recv, image_sem)
    valid_left = lax.rem(lane16 + 32 * q_left, LANES) < WIDTH
    valid_right = lax.rem(lane16 + 32 * q_right, LANES) < WIDTH
    image = image_send[col]
    for o in range(COLS - 1):
        image = image + image_recv[o]
    image = jnp.where(valid_left, image, 0.0)

    def sums_rs_send(side, values, basis):
        for i in range(3):
            p_local[side, 64 * i : 64 * i + 64, :] = dot_nt(values, basis[128 * i : 128 * i + 128, :])
        p_local[side, 192:256, 0:BLOCK] = dot_nt(values, values)
        p_local[side, 192:256, BLOCK:LANES] = jnp.zeros((BLOCK, LANES - BLOCK), F32)
        send_row(lambda o, peer: p_local.at[side, pl.ds(pl.multiple_of(8 * peer, 8), 8)], lambda o: p_rs.at[side, o - 1], p_rs_sem.at[side], send_sem.at[8 + side])

    def sums_ar_send(side):
        wait_bytes(p_rs.at[side], p_rs_sem.at[side])
        total = p_local[side, pl.ds(pl.multiple_of(8 * row, 8), 8), :]
        for o in range(ROWS - 1):
            total = total + p_rs[side, o]
        p_ar[side, col] = total
        send_col(lambda o, peer: p_ar.at[side, col], lambda o: p_ar.at[side, col], p_ar_sem.at[side], send_sem.at[10 + side])

    def sums_ag_send(side):
        wait_bytes(p_ar.at[side, pl.ds(0, COLS - 1)], p_ar_sem.at[side])
        total = p_ar[side, 0]
        for c in range(1, COLS):
            total = total + p_ar[side, c]
        p_all[side, row] = total
        send_row(lambda o, peer: p_all.at[side, row], lambda o: p_all.at[side, row], p_ag_sem.at[side], send_sem.at[12 + side])

    def sums_wait(side):
        wait_bytes(p_all.at[side, pl.ds(0, ROWS - 1)], p_ag_sem.at[side])

    def finish(side, values, basis):
        sums = [jnp.concatenate([p_all[side, 8 * i + t] for t in range(8)], axis=0) for i in range(4)]
        coefficients = [sums[i] * (1.0 / N) for i in range(3)]
        gram_blocks = {}
        k = 0
        for i in range(3):
            for j in range(i + 1):
                gram_blocks[(i, j)] = jnp.concatenate([g_all[side, (128 * k + 8 * t) // 24, (128 * k + 8 * t) % 24 : (128 * k + 8 * t) % 24 + 8, :] for t in range(16)], axis=0)
                k += 1
        gram = sums[3][:, 0:BLOCK]
        for j in range(3):
            along = 2.0 * sums[j]
            for i in range(3):
                if i >= j:
                    along = along - dot_nn(coefficients[i], gram_blocks[(i, j)])
                else:
                    along = along - dot_nt(coefficients[i], gram_blocks[(j, i)])
            gram = gram - dot_nt(along, coefficients[j])
        projected = values
        for i in range(3):
            projected = projected - dot_nn(coefficients[i], basis[128 * i : 128 * i + 128, :])
        eliminated = cholesky_and_inverse(gram * (1.0 / N))
        new_block = dot_nn(eliminated[:, BLOCK:LANES], projected)
        upper = jnp.where(lane16 >= lax.broadcasted_iota(jnp.int32, (BLOCK, LANES), 0), eliminated, 0.0)
        return new_block, upper

    def write_factor(side, upper):
        factors_out[side] = jnp.transpose(upper)[0:BLOCK, :]

    sums_rs_send(0, image, left_set)
    gram_ar_send(0)
    sums_ar_send(0)
    gram_ag_send(0)
    sums_ag_send(0)
    gram_wait(0)
    sums_wait(0)
    gram_rs_send(1)
    left_new, left_upper = finish(0, image, left_set)
    u_slots[col] = left_new.astype(BF16)
    send_col(lambda o, peer: u_slots.at[col], lambda o: u_slots.at[col], u_sem, send_sem.at[14])
    gram_ar_send(1)
    left_out[...] = pltpu.roll(left_new, left_back, 1)[:, 0:WIDTH]
    write_factor(0, left_upper)

    wait_bytes(u_slots.at[pl.ds(0, COLS - 1)], u_sem)
    joined(u_slots, u_all, COLS)
    for group in range(8):
        part = lax.dot_general(
            u_all[...], matrix[:, 384 * group : 384 * group + 384], (((1,), (0,)), ((), ())), preferred_element_type=F32
        )
        for k, piece in enumerate(pieces(part)):
            co_send[4 * group + k] = piece.astype(BF16)
    send_row(lambda o, peer: co_send.at[peer], lambda o: co_recv.at[o - 1], co_sem, send_sem.at[15])
    wait_bytes(co_recv, co_sem)
    coimage = co_send[row].astype(F32)
    for o in range(ROWS - 1):
        coimage = coimage + co_recv[o].astype(F32)
    coimage = jnp.where(valid_right, coimage, 0.0)
    sums_rs_send(1, coimage, right_set)
    sums_ar_send(1)
    gram_ag_send(1)
    sums_ag_send(1)
    gram_wait(1)
    sums_wait(1)
    right_new, right_upper = finish(1, coimage, right_set)
    right_out[...] = pltpu.roll(right_new, right_back, 1)[:, 0:WIDTH]
    write_factor(1, right_upper)

    wait_bytes(b_slots.at[pl.ds(0, ROWS - 1)], send_sem.at[0])
    wait_bytes(image_recv, send_sem.at[7])
    wait_bytes(u_slots.at[pl.ds(0, COLS - 1)], send_sem.at[14])
    wait_bytes(co_recv, send_sem.at[15])
    for side in range(2):
        wait_bytes(g_rs.at[side], send_sem.at[1 + side])
        wait_bytes(g_ar.at[side, pl.ds(0, COLS - 1)], send_sem.at[3 + side])
        wait_bytes(g_all.at[side, pl.ds(0, ROWS - 1)], send_sem.at[5 + side])
        wait_bytes(p_rs.at[side], send_sem.at[8 + side])
        wait_bytes(p_ar.at[side, pl.ds(0, COLS - 1)], send_sem.at[10 + side])
        wait_bytes(p_all.at[side, pl.ds(0, ROWS - 1)], send_sem.at[12 + side])


def shards(matrix, left_basis, right_basis, right_block):
    any_space = pl.BlockSpec(memory_space=pl.ANY)
    in_vmem = pl.BlockSpec(memory_space=pltpu.VMEM)
    dma = pltpu.SemaphoreType.DMA
    return pl.pallas_call(
        kernel,
        out_shape=(
            jax.ShapeDtypeStruct((BLOCK, WIDTH), F32),
            jax.ShapeDtypeStruct((BLOCK, WIDTH), F32),
            jax.ShapeDtypeStruct((2, BLOCK, BLOCK), F32),
        ),
        in_specs=[any_space] * 4,
        out_specs=(in_vmem, in_vmem, in_vmem),
        scratch_shapes=[
            pltpu.VMEM((768, 3072), BF16),
            pltpu.VMEM((PRIOR_ROWS, WIDTH), F32),
            pltpu.VMEM((PRIOR_ROWS, WIDTH), F32),
            pltpu.VMEM((BLOCK, WIDTH), F32),
            pltpu.VMEM((SET_ROWS, LANES), F32),
            pltpu.VMEM((SET_ROWS, LANES), F32),
            pltpu.VMEM((ROWS, BLOCK, LANES), BF16),
            pltpu.VMEM((BLOCK, 3072), BF16),
            pltpu.VMEM((COLS, BLOCK, LANES), F32),
            pltpu.VMEM((COLS - 1, BLOCK, LANES), F32),
            pltpu.VMEM((COLS, BLOCK, LANES), BF16),
            pltpu.VMEM((BLOCK, 768), BF16),
            pltpu.VMEM((ROWS, BLOCK, LANES), BF16),
            pltpu.VMEM((ROWS - 1, BLOCK, LANES), BF16),
            pltpu.VMEM((2, 256, LANES), F32),
            pltpu.VMEM((2, ROWS - 1, 8, LANES), F32),
            pltpu.VMEM((2, COLS, 8, LANES), F32),
            pltpu.VMEM((2, ROWS, 8, LANES), F32),
            pltpu.VMEM((2, 768, LANES), F32),
            pltpu.VMEM((2, ROWS - 1, 24, LANES), F32),
            pltpu.VMEM((2, COLS, 24, LANES), F32),
            pltpu.VMEM((2, ROWS, 24, LANES), F32),
            dma((4,)), dma((16,)), dma(()), dma(()), dma(()), dma(()),
            dma((2,)), dma((2,)), dma((2,)), dma((2,)), dma((2,)), dma((2,)),
        ],
        compiler_params=pltpu.CompilerParams(
            collective_id=0, has_side_effects=True, vmem_limit_bytes=48 * 1024 * 1024
        ),
        cost_estimate=pl.CostEstimate(flops=700_000_000, bytes_accessed=8_000_000, transcendentals=0),
    )(matrix, left_basis, right_basis, right_block)


def solution(mesh):
    in_specs = (
        P("row", "col"),
        P(None, ("row", "col")),
        P(None, ("col", "row")),
        P(None, ("col", "row")),
    )
    out_specs = (P(None, ("row", "col")), P(None, ("col", "row")), P())
    return jax.shard_map(shards, mesh=mesh, in_specs=in_specs, out_specs=out_specs, check_vma=False)
```

```python
import jax
import jax.numpy as jnp
from jax import lax
from jax.experimental import pallas as pl
from jax.experimental.pallas import tpu as pltpu
from jax.sharding import PartitionSpec as P

N = 24576
BLOCK = 64
PRIOR_ROWS = 320
SET_ROWS = 384
COLS = 8
ROWS = 32
WIDTH = 96
LANES = 128
MESH = pl.DeviceIdType.MESH
F32 = jnp.float32
BF16 = jnp.bfloat16
highest_precision = lax.Precision.HIGHEST


def dot_nn(first, second):
    return lax.dot_general(first, second, (((1,), (0,)), ((), ())), precision=highest_precision, preferred_element_type=F32)


def dot_nt(first, second):
    return lax.dot_general(first, second, (((1,), (1,)), ((), ())), precision=highest_precision, preferred_element_type=F32)


def wait_bytes(ref, sem):
    pltpu.make_async_copy(ref, ref, sem).wait()


def lanes_of(shape):
    return lax.broadcasted_iota(jnp.int32, shape, 1)


def cholesky_and_inverse(gram):
    lane = lanes_of((8, LANES))
    sub = lax.broadcasted_iota(jnp.int32, (8, LANES), 0)

    def spread(values):
        return jnp.broadcast_to(values, (8, LANES))

    blocks = []
    for k in range(8):
        unit = jnp.where(lane == sub + (BLOCK + 8 * k), 1.0, 0.0)
        padded = jnp.concatenate([gram[8 * k : 8 * k + 8, :], jnp.zeros((8, BLOCK), F32)], axis=1)
        blocks.append(padded + unit)
    for b in range(8):
        columns = [[spread(blocks[k][:, 8 * b + i : 8 * b + i + 1]) for k in range(b, 8)] for i in range(8)]
        for i in range(8):
            inverse = lax.rsqrt(spread(columns[i][0][i : i + 1, :]))
            lower = [column * inverse for column in columns[i]]
            row = spread(blocks[b][i : i + 1, :]) * inverse
            for m in range(i + 1, 8):
                weight = spread(lower[0][m : m + 1, :])
                columns[m] = [column - below * weight for column, below in zip(columns[m], lower)]
            updated = blocks[b] - lower[0] * row
            blocks[b] = jnp.where(sub > i, updated, jnp.where(sub == i, row, blocks[b]))
            for k in range(b + 1, 8):
                blocks[k] = blocks[k] - lower[k - b] * row
    return jnp.concatenate(blocks, axis=0)


def kernel(
    matrix_hbm, left_hbm, right_hbm, block_hbm,
    left_out, right_out, factors_out,
    matrix, left_in, right_in, block_in,
    turned, left_set, right_set,
    b_slots, b_all, image_sum, image_send, image_recv,
    u_slots, u_all, co_send, co_recv,
    p_local, p_rs, p_ar, p_all,
    g_local, g_rs, g_ar, g_all, weights,
    load_sem, send_sem, b_sem, image_sem, u_sem, co_sem,
    p_rs_sem, p_ar_sem, p_ag_sem, g_rs_sem, g_ar_sem, g_ag_sem,
):
    col = lax.axis_index("col")
    row = lax.axis_index("row")
    q_left = lax.rem(col, 4)
    q_right = lax.rem(row, 4)

    def row_peer(o):
        return lax.rem(row + o, ROWS)

    def col_peer(o):
        return lax.rem(col + o, COLS)

    barrier = pltpu.get_barrier_semaphore()

    def greet_row(o, carry):
        pl.semaphore_signal(barrier, inc=1, device_id=(col, row_peer(o)), device_id_type=MESH)
        return carry

    def greet_col(o, carry):
        pl.semaphore_signal(barrier, inc=1, device_id=(col_peer(o), row), device_id_type=MESH)
        return carry

    load_block = pltpu.make_async_copy(block_hbm, block_in, load_sem.at[0])
    load_left = pltpu.make_async_copy(left_hbm, left_in, load_sem.at[1])
    load_right = pltpu.make_async_copy(right_hbm, right_in, load_sem.at[2])
    load_matrix = pltpu.make_async_copy(matrix_hbm, matrix, load_sem.at[3])
    load_block.start()
    lax.fori_loop(1, ROWS, greet_row, 0)
    lax.fori_loop(1, COLS, greet_col, 0)
    load_left.start()
    load_right.start()
    load_matrix.start()

    def send_row(source, target, sem, send):
        def body(k, carry):
            o = lax.rem(k + 15, ROWS - 1) + 1
            peer = row_peer(o)
            pltpu.make_async_remote_copy(
                src_ref=source(o, peer), dst_ref=target(o), send_sem=send, recv_sem=sem,
                device_id=(col, peer), device_id_type=MESH,
            ).start()
            return carry

        lax.fori_loop(0, ROWS - 1, body, 0)

    def send_col(source, target, sem, send):
        def body(k, carry):
            o = lax.rem(k + 3, COLS - 1) + 1
            peer = col_peer(o)
            pltpu.make_async_remote_copy(
                src_ref=source(o, peer), dst_ref=target(o), send_sem=send, recv_sem=sem,
                device_id=(peer, row), device_id_type=MESH,
            ).start()
            return carry

        lax.fori_loop(0, COLS - 1, body, 0)

    right_shift = lax.rem(96 * q_right, LANES)
    right_back = lax.rem(32 * q_right, LANES)
    left_back = lax.rem(32 * q_left, LANES)

    turned[...] = jnp.zeros_like(turned)
    load_block.wait()
    left_set[0:BLOCK, :] = jnp.zeros((BLOCK, LANES), F32)
    left_set[0:BLOCK, 0:WIDTH] = block_in[...]
    turned_block = pltpu.roll(left_set[0:BLOCK, :], right_shift, 1)
    b_slots[row] = turned_block.astype(BF16)
    pl.semaphore_wait(barrier, ROWS + COLS - 2)
    plane, within = row // 8, lax.rem(row, 8)

    def own_plane_peer(w):
        return plane * 8 + lax.rem(within + w, 8)

    def other_plane_peer(y, w):
        return lax.rem(plane + y, 4) * 8 + lax.rem(within + w, 8)

    def send_block(peer, y):
        pltpu.make_async_remote_copy(
            src_ref=b_slots.at[row], dst_ref=b_slots.at[row], send_sem=send_sem.at[0], recv_sem=b_sem.at[y],
            device_id=(col, peer), device_id_type=MESH,
        ).start()

    def send_block_near(w, carry):
        send_block(own_plane_peer(w), 0)
        return carry

    lax.fori_loop(1, 8, send_block_near, 0)
    for y in (1, 3, 2):
        def send_block_far(w, carry, y=y):
            send_block(other_plane_peer(y, w), y)
            return carry

        lax.fori_loop(0, 8, send_block_far, 0)

    def turn(basis, q, out):
        for k in range(3):
            place = pl.multiple_of(32 * lax.rem(k + 3 * q, 4), 32)
            turned[pl.ds(place, 32), 0:PRIOR_ROWS] = basis[32 * k : 32 * k + 32, :]
        turned[pl.ds(pl.multiple_of(32 * lax.rem(3 + 3 * q, 4), 32), 32), :] = jnp.zeros((32, SET_ROWS), F32)
        for i in range(3):
            out[128 * i : 128 * i + 128, :] = jnp.transpose(turned[:, 128 * i : 128 * i + 128])

    load_left.wait()
    turn(left_in, q_left, left_set)
    load_right.wait()
    turn(right_in, q_right, right_set)
    right_set[PRIOR_ROWS:SET_ROWS, :] = turned_block

    def start_gram(side, basis):
        k = 0
        for i in range(3):
            for j in range(i + 1):
                block = dot_nt(basis[128 * i : 128 * i + 128, :], basis[128 * j : 128 * j + 128, :])
                g_local[side, 128 * k : 128 * k + 128, :] = block
                k += 1

    def gram_rs_send(side):
        send_row(lambda o, peer: g_local.at[side, pl.ds(pl.multiple_of(24 * peer, 8), 24)], lambda o: g_rs.at[side, o - 1], g_rs_sem.at[side], send_sem.at[1 + side])

    def gram_ar_send(side):
        wait_bytes(g_rs.at[side], g_rs_sem.at[side])
        total = g_local[side, pl.ds(pl.multiple_of(24 * row, 8), 24), :]
        for o in range(ROWS - 1):
            total = total + g_rs[side, o]
        g_ar[side, col] = total
        send_col(lambda o, peer: g_ar.at[side, col], lambda o: g_ar.at[side, col], g_ar_sem.at[side], send_sem.at[3 + side])

    def gram_ag_send(side):
        wait_bytes(g_ar.at[side, pl.ds(0, COLS - 1)], g_ar_sem.at[side])
        total = g_ar[side, 0]
        for c in range(1, COLS):
            total = total + g_ar[side, c]
        g_all[side, row] = total
        send_row(lambda o, peer: g_all.at[side, row], lambda o: g_all.at[side, row], g_ag_sem.at[side], send_sem.at[5 + side])

    def gram_wait(side):
        wait_bytes(g_all.at[side, pl.ds(0, ROWS - 1)], g_ag_sem.at[side])
        k = 0
        for i in range(3):
            for j in range(i + 1):
                for t in range(16):
                    at = 128 * k + 8 * t
                    weights[128 * i + 8 * t : 128 * i + 8 * t + 8, 128 * j : 128 * j + 128] = g_all[side, at // 24, at % 24 : at % 24 + 8, :] * (-1.0 / N / N)
                block = weights[128 * i : 128 * i + 128, 128 * j : 128 * j + 128]
                if i == j:
                    same = lanes_of((128, LANES)) == lax.broadcasted_iota(jnp.int32, (128, LANES), 0)
                    weights[128 * i : 128 * i + 128, 128 * j : 128 * j + 128] = block + jnp.where(same, 2.0 / N, 0.0)
                else:
                    weights[128 * j : 128 * j + 128, 128 * i : 128 * i + 128] = jnp.transpose(block)
                k += 1

    start_gram(0, left_set)

    lane16 = lanes_of((BLOCK, LANES))

    def joined(slots):
        chunks = []
        for group in range(2):
            first, second, third, fourth = (slots(4 * group + k).astype(F32) for k in range(4))
            chunks.append(jnp.where(lane16 < 96, first, second).astype(BF16))
            chunks.append(jnp.where(lane16 < 64, second, third).astype(BF16))
            chunks.append(jnp.where(lane16 < 32, third, fourth).astype(BF16))
        return jnp.concatenate(chunks, axis=1)

    def pieces(values):
        first, second, third = (values[:, 128 * k : 128 * k + 128] for k in range(3))
        return (first, jnp.where(lane16 < 64, second, first), jnp.where(lane16 < 64, third, second), third)

    load_matrix.wait()
    for y in (0, 1, 3, 2):
        wait_bytes(b_slots.at[pl.ds(0, 7 if y == 0 else 8)], b_sem.at[y])
        source = lax.rem(plane + (4 - y), 4)
        b_all[...] = joined(lambda k: b_slots[8 * source + k])
        if y == 2:
            gram_rs_send(0)
        part = lax.dot_general(
            b_all[...], matrix[:, pl.ds(pl.multiple_of(768 * source, 768), 768)], (((1,), (1,)), ((), ())), preferred_element_type=F32
        )
        if y == 0:
            image_sum[...] = part
        else:
            image_sum[...] += part
    for half in range(2):
        for k, piece in enumerate(pieces(image_sum[:, 384 * half : 384 * half + 384])):
            image_send[4 * half + k] = piece
    send_col(lambda o, peer: image_send.at[peer], lambda o: image_recv.at[o - 1], image_sem, send_sem.at[7])
    start_gram(1, right_set)
    wait_bytes(image_recv, image_sem)
    valid_left = lax.rem(lane16 + 32 * q_left, LANES) < WIDTH
    valid_right = lax.rem(lane16 + 32 * q_right, LANES) < WIDTH
    image = image_send[col]
    for o in range(COLS - 1):
        image = image + image_recv[o]
    image = jnp.where(valid_left, image, 0.0)

    def sums_rs_send(side, values, basis):
        for i in range(3):
            p_local[side, 64 * i : 64 * i + 64, :] = dot_nt(values, basis[128 * i : 128 * i + 128, :])
        p_local[side, 192:256, 0:BLOCK] = dot_nt(values, values)
        p_local[side, 192:256, BLOCK:LANES] = jnp.zeros((BLOCK, LANES - BLOCK), F32)
        send_row(lambda o, peer: p_local.at[side, pl.ds(pl.multiple_of(8 * peer, 8), 8)], lambda o: p_rs.at[side, o - 1], p_rs_sem.at[side], send_sem.at[8 + side])

    def sums_ar_send(side):
        wait_bytes(p_rs.at[side], p_rs_sem.at[side])
        total = p_local[side, pl.ds(pl.multiple_of(8 * row, 8), 8), :]
        for o in range(ROWS - 1):
            total = total + p_rs[side, o]
        p_ar[side, col] = total
        send_col(lambda o, peer: p_ar.at[side, col], lambda o: p_ar.at[side, col], p_ar_sem.at[side], send_sem.at[10 + side])

    def sums_ag_send(side):
        wait_bytes(p_ar.at[side, pl.ds(0, COLS - 1)], p_ar_sem.at[side])
        total = p_ar[side, 0]
        for c in range(1, COLS):
            total = total + p_ar[side, c]
        p_all[side, row] = total
        send_row(lambda o, peer: p_all.at[side, row], lambda o: p_all.at[side, row], p_ag_sem.at[side], send_sem.at[12 + side])

    def sums_wait(side):
        wait_bytes(p_all.at[side, pl.ds(0, ROWS - 1)], p_ag_sem.at[side])

    def finish(side, values, basis):
        sums = [jnp.concatenate([p_all[side, 8 * i + t] for t in range(8)], axis=0) for i in range(4)]
        joint = jnp.concatenate(sums[0:3], axis=1)
        gram = sums[3][:, 0:BLOCK] - dot_nt(dot_nn(joint, weights[...]), joint)
        projected = values - dot_nn(joint * (1.0 / N), basis[...])
        eliminated = cholesky_and_inverse(gram * (1.0 / N))
        new_block = dot_nn(eliminated[:, BLOCK:LANES], projected)
        upper = jnp.where(lane16 >= lax.broadcasted_iota(jnp.int32, (BLOCK, LANES), 0), eliminated, 0.0)
        return new_block, upper

    def write_factor(side, upper):
        factors_out[side] = jnp.transpose(upper)[0:BLOCK, :]

    sums_rs_send(0, image, left_set)
    gram_ar_send(0)
    sums_ar_send(0)
    gram_ag_send(0)
    sums_ag_send(0)
    gram_wait(0)
    sums_wait(0)
    gram_rs_send(1)
    left_new, left_upper = finish(0, image, left_set)
    u_slots[col] = left_new.astype(BF16)
    send_col(lambda o, peer: u_slots.at[col], lambda o: u_slots.at[col], u_sem, send_sem.at[14])
    gram_ar_send(1)
    left_out[...] = pltpu.roll(left_new, left_back, 1)[:, 0:WIDTH]
    write_factor(0, left_upper)

    wait_bytes(u_slots.at[pl.ds(0, COLS - 1)], u_sem)
    u_all[...] = joined(lambda k: u_slots[k])

    def send_piece(peer, y):
        pltpu.make_async_remote_copy(
            src_ref=co_send.at[peer], dst_ref=co_recv.at[8 * y + within], send_sem=send_sem.at[15], recv_sem=co_sem.at[y],
            device_id=(col, peer), device_id_type=MESH,
        ).start()

    for y in (2, 1, 3, 0):
        target = lax.rem(plane + y, 4)
        part = lax.dot_general(
            u_all[...], matrix[:, pl.ds(pl.multiple_of(768 * target, 768), 768)], (((1,), (0,)), ((), ())), preferred_element_type=F32
        )
        for half in range(2):
            for k, piece in enumerate(pieces(part[:, 384 * half : 384 * half + 384])):
                co_send[8 * target + 4 * half + k] = piece.astype(BF16)
        if y == 0:
            def send_piece_near(w, carry):
                send_piece(own_plane_peer(w), 0)
                return carry

            lax.fori_loop(1, 8, send_piece_near, 0)
        else:
            def send_piece_far(w, carry, y=y):
                send_piece(other_plane_peer(y, w), y)
                return carry

            lax.fori_loop(0, 8, send_piece_far, 0)
    co_recv[within] = co_send[row]
    coimage = jnp.zeros((BLOCK, LANES), F32)
    for y in (0, 1, 3, 2):
        wait_bytes(co_recv.at[pl.ds(8 * y, 7 if y == 0 else 8)], co_sem.at[y])
        for w in range(8):
            coimage = coimage + co_recv[8 * y + w].astype(F32)
    coimage = jnp.where(valid_right, coimage, 0.0)
    sums_rs_send(1, coimage, right_set)
    sums_ar_send(1)
    gram_ag_send(1)
    sums_ag_send(1)
    gram_wait(1)
    sums_wait(1)
    right_new, right_upper = finish(1, coimage, right_set)
    right_out[...] = pltpu.roll(right_new, right_back, 1)[:, 0:WIDTH]
    write_factor(1, right_upper)

    wait_bytes(b_slots.at[pl.ds(0, ROWS - 1)], send_sem.at[0])
    wait_bytes(image_recv, send_sem.at[7])
    wait_bytes(u_slots.at[pl.ds(0, COLS - 1)], send_sem.at[14])
    wait_bytes(co_recv.at[pl.ds(0, ROWS - 1)], send_sem.at[15])
    for side in range(2):
        wait_bytes(g_rs.at[side], send_sem.at[1 + side])
        wait_bytes(g_ar.at[side, pl.ds(0, COLS - 1)], send_sem.at[3 + side])
        wait_bytes(g_all.at[side, pl.ds(0, ROWS - 1)], send_sem.at[5 + side])
        wait_bytes(p_rs.at[side], send_sem.at[8 + side])
        wait_bytes(p_ar.at[side, pl.ds(0, COLS - 1)], send_sem.at[10 + side])
        wait_bytes(p_all.at[side, pl.ds(0, ROWS - 1)], send_sem.at[12 + side])


def shards(matrix, left_basis, right_basis, right_block):
    in_hbm = pl.BlockSpec(memory_space=pltpu.HBM)
    in_vmem = pl.BlockSpec(memory_space=pltpu.VMEM)
    dma = pltpu.SemaphoreType.DMA
    return pl.pallas_call(
        kernel,
        out_shape=(
            jax.ShapeDtypeStruct((BLOCK, WIDTH), F32),
            jax.ShapeDtypeStruct((BLOCK, WIDTH), F32),
            jax.ShapeDtypeStruct((2, BLOCK, BLOCK), F32),
        ),
        in_specs=[in_hbm] * 4,
        out_specs=(in_vmem, in_vmem, in_vmem),
        scratch_shapes=[
            pltpu.VMEM((768, 3072), BF16),
            pltpu.VMEM((WIDTH, PRIOR_ROWS), F32),
            pltpu.VMEM((WIDTH, PRIOR_ROWS), F32),
            pltpu.VMEM((BLOCK, WIDTH), F32),
            pltpu.VMEM((LANES, SET_ROWS), F32),
            pltpu.VMEM((SET_ROWS, LANES), F32),
            pltpu.VMEM((SET_ROWS, LANES), F32),
            pltpu.VMEM((ROWS, BLOCK, LANES), BF16),
            pltpu.VMEM((BLOCK, 768), BF16),
            pltpu.VMEM((BLOCK, 768), F32),
            pltpu.VMEM((COLS, BLOCK, LANES), F32),
            pltpu.VMEM((COLS - 1, BLOCK, LANES), F32),
            pltpu.VMEM((COLS, BLOCK, LANES), BF16),
            pltpu.VMEM((BLOCK, 768), BF16),
            pltpu.VMEM((ROWS, BLOCK, LANES), BF16),
            pltpu.VMEM((ROWS, BLOCK, LANES), BF16),
            pltpu.VMEM((2, 256, LANES), F32),
            pltpu.VMEM((2, ROWS - 1, 8, LANES), F32),
            pltpu.VMEM((2, COLS, 8, LANES), F32),
            pltpu.VMEM((2, ROWS, 8, LANES), F32),
            pltpu.VMEM((2, 768, LANES), F32),
            pltpu.VMEM((2, ROWS - 1, 24, LANES), F32),
            pltpu.VMEM((2, COLS, 24, LANES), F32),
            pltpu.VMEM((2, ROWS, 24, LANES), F32),
            pltpu.VMEM((SET_ROWS, SET_ROWS), F32),
            dma((4,)), dma((16,)), dma((4,)), dma(()), dma(()), dma((4,)),
            dma((2,)), dma((2,)), dma((2,)), dma((2,)), dma((2,)), dma((2,)),
        ],
        compiler_params=pltpu.CompilerParams(
            collective_id=0, has_side_effects=True, vmem_limit_bytes=(53 * 1024 + 768) * 1024
        ),
        cost_estimate=pl.CostEstimate(flops=700_000_000, bytes_accessed=8_000_000, transcendentals=0),
    )(matrix, left_basis.T, right_basis.T, right_block)


def solution(mesh):
    in_specs = (
        P("row", "col"),
        P(None, ("row", "col")),
        P(None, ("col", "row")),
        P(None, ("col", "row")),
    )
    out_specs = (P(None, ("row", "col")), P(None, ("col", "row")), P())
    return jax.shard_map(shards, mesh=mesh, in_specs=in_specs, out_specs=out_specs, check_vma=False)
```

```python
import jax
import jax.numpy as jnp
from jax import lax
from jax.experimental import pallas as pl
from jax.experimental.pallas import tpu as pltpu
from jax.sharding import PartitionSpec as P

N = 24576
BLOCK = 64
PRIOR_ROWS = 320
SET_ROWS = 384
COLS = 8
ROWS = 32
WIDTH = 96
LANES = 128
MESH = pl.DeviceIdType.MESH
F32 = jnp.float32
BF16 = jnp.bfloat16
highest_precision = lax.Precision.HIGHEST


def dot_nn(first, second):
    return lax.dot_general(first, second, (((1,), (0,)), ((), ())), precision=highest_precision, preferred_element_type=F32)


def dot_nt(first, second):
    return lax.dot_general(first, second, (((1,), (1,)), ((), ())), precision=highest_precision, preferred_element_type=F32)


def wait_bytes(ref, sem):
    pltpu.make_async_copy(ref, ref, sem).wait()


def lanes_of(shape):
    return lax.broadcasted_iota(jnp.int32, shape, 1)


def valid_lanes(shape, q):
    return lax.rem(lanes_of(shape) + 32 * q, LANES) < WIDTH


def pack(values, q):
    moved = jnp.concatenate([pltpu.roll(values[48:64, :], 32 * (3 - k), 1) for k in range(3)], axis=0)
    return jnp.where(valid_lanes((48, LANES), q), values[0:48, :], moved)


def unpack(packed, q):
    group = lax.rem(lanes_of((16, LANES)) + 32 * q, LANES)
    back = [pltpu.roll(packed[16 * k : 16 * k + 16, :], 32 * (1 + k), 1) for k in range(3)]
    last = jnp.where(group < 32, back[0], jnp.where(group < 64, back[1], back[2]))
    return jnp.concatenate([packed, last], axis=0)


def cholesky_and_inverse(gram):
    lane = lanes_of((8, LANES))
    sub = lax.broadcasted_iota(jnp.int32, (8, LANES), 0)

    def spread(values):
        return jnp.broadcast_to(values, (8, LANES))

    blocks = []
    for k in range(8):
        unit = jnp.where(lane == sub + (BLOCK + 8 * k), 1.0, 0.0)
        padded = jnp.concatenate([gram[8 * k : 8 * k + 8, :], jnp.zeros((8, BLOCK), F32)], axis=1)
        blocks.append(padded + unit)
    for b in range(8):
        columns = [[spread(blocks[k][:, 8 * b + i : 8 * b + i + 1]) for k in range(b, 8)] for i in range(8)]
        for i in range(8):
            inverse = lax.rsqrt(spread(columns[i][0][i : i + 1, :]))
            lower = [column * inverse for column in columns[i]]
            row = spread(blocks[b][i : i + 1, :]) * inverse
            for m in range(i + 1, 8):
                weight = spread(lower[0][m : m + 1, :])
                columns[m] = [column - below * weight for column, below in zip(columns[m], lower)]
            updated = blocks[b] - lower[0] * row
            blocks[b] = jnp.where(sub > i, updated, jnp.where(sub == i, row, blocks[b]))
            for k in range(b + 1, 8):
                blocks[k] = blocks[k] - lower[k - b] * row
    return jnp.concatenate(blocks, axis=0)


def kernel(
    matrix_hbm, left_hbm, right_hbm, block_hbm,
    left_out, right_out, factors_out,
    matrix, left_in, right_in, block_in,
    turned, left_set, right_set,
    b_slots, b_all, image_sum, image_send, image_recv,
    u_slots, u_all, co_send, co_recv,
    p_local, p_rs, p_ar, p_all,
    g_local, g_rs, g_ar, g_all, weights,
    load_sem, send_sem, b_sem, image_sem, u_sem, co_sem,
    p_rs_sem, p_ar_sem, p_ag_sem, g_rs_sem, g_ar_sem, g_ag_sem,
):
    col = lax.axis_index("col")
    row = lax.axis_index("row")
    q_left = lax.rem(col, 4)
    q_right = lax.rem(row, 4)

    def row_peer(o):
        return lax.rem(row + o, ROWS)

    def col_peer(o):
        return lax.rem(col + o, COLS)

    barrier = pltpu.get_barrier_semaphore()

    def greet_row(o, carry):
        pl.semaphore_signal(barrier, inc=1, device_id=(col, row_peer(o)), device_id_type=MESH)
        return carry

    def greet_col(o, carry):
        pl.semaphore_signal(barrier, inc=1, device_id=(col_peer(o), row), device_id_type=MESH)
        return carry

    load_block = pltpu.make_async_copy(block_hbm, block_in, load_sem.at[0])
    load_left = pltpu.make_async_copy(left_hbm, left_in, load_sem.at[1])
    load_right = pltpu.make_async_copy(right_hbm, right_in, load_sem.at[2])
    load_matrix = pltpu.make_async_copy(matrix_hbm, matrix, load_sem.at[3])
    load_block.start()
    lax.fori_loop(1, ROWS, greet_row, 0)
    lax.fori_loop(1, COLS, greet_col, 0)
    load_left.start()
    load_right.start()
    load_matrix.start()

    def send_row(source, target, sem, send):
        def body(k, carry):
            o = lax.rem(k + 15, ROWS - 1) + 1
            peer = row_peer(o)
            pltpu.make_async_remote_copy(
                src_ref=source(o, peer), dst_ref=target(o), send_sem=send, recv_sem=sem,
                device_id=(col, peer), device_id_type=MESH,
            ).start()
            return carry

        lax.fori_loop(0, ROWS - 1, body, 0)

    def send_col(source, target, sem, send):
        def body(k, carry):
            o = lax.rem(k + 3, COLS - 1) + 1
            peer = col_peer(o)
            pltpu.make_async_remote_copy(
                src_ref=source(o, peer), dst_ref=target(o), send_sem=send, recv_sem=sem,
                device_id=(peer, row), device_id_type=MESH,
            ).start()
            return carry

        lax.fori_loop(0, COLS - 1, body, 0)

    right_shift = lax.rem(96 * q_right, LANES)
    right_back = lax.rem(32 * q_right, LANES)
    left_back = lax.rem(32 * q_left, LANES)

    turned[...] = jnp.zeros_like(turned)
    load_block.wait()
    left_set[0:BLOCK, :] = jnp.zeros((BLOCK, LANES), F32)
    left_set[0:BLOCK, 0:WIDTH] = block_in[...]
    turned_block = pltpu.roll(left_set[0:BLOCK, :], right_shift, 1)
    b_slots[row] = pack(turned_block, q_right).astype(BF16)
    pl.semaphore_wait(barrier, ROWS + COLS - 2)
    plane, within = row // 8, lax.rem(row, 8)

    def own_plane_peer(w):
        return plane * 8 + lax.rem(within + w, 8)

    def other_plane_peer(y, w):
        return lax.rem(plane + y, 4) * 8 + lax.rem(within + w, 8)

    def send_block(peer, y):
        pltpu.make_async_remote_copy(
            src_ref=b_slots.at[row], dst_ref=b_slots.at[row], send_sem=send_sem.at[0], recv_sem=b_sem.at[y],
            device_id=(col, peer), device_id_type=MESH,
        ).start()

    def send_block_near(w, carry):
        send_block(own_plane_peer(w), 0)
        return carry

    lax.fori_loop(1, 8, send_block_near, 0)
    for y in (1, 3, 2):
        def send_block_far(w, carry, y=y):
            send_block(other_plane_peer(y, w), y)
            return carry

        lax.fori_loop(0, 8, send_block_far, 0)

    def turn(basis, q, out):
        for k in range(3):
            place = pl.multiple_of(32 * lax.rem(k + 3 * q, 4), 32)
            turned[pl.ds(place, 32), 0:PRIOR_ROWS] = basis[32 * k : 32 * k + 32, :]
        turned[pl.ds(pl.multiple_of(32 * lax.rem(3 + 3 * q, 4), 32), 32), :] = jnp.zeros((32, SET_ROWS), F32)
        for i in range(3):
            out[128 * i : 128 * i + 128, :] = jnp.transpose(turned[:, 128 * i : 128 * i + 128])

    load_left.wait()
    turn(left_in, q_left, left_set)
    load_right.wait()
    turn(right_in, q_right, right_set)
    right_set[PRIOR_ROWS:SET_ROWS, :] = turned_block

    def start_gram(side, basis):
        k = 0
        for i in range(3):
            for j in range(i + 1):
                block = dot_nt(basis[128 * i : 128 * i + 128, :], basis[128 * j : 128 * j + 128, :])
                g_local[side, 128 * k : 128 * k + 128, :] = block
                k += 1

    def gram_rs_send(side):
        send_row(lambda o, peer: g_local.at[side, pl.ds(pl.multiple_of(24 * peer, 8), 24)], lambda o: g_rs.at[side, o - 1], g_rs_sem.at[side], send_sem.at[1 + side])

    def gram_ar_send(side):
        wait_bytes(g_rs.at[side], g_rs_sem.at[side])
        total = g_local[side, pl.ds(pl.multiple_of(24 * row, 8), 24), :]
        for o in range(ROWS - 1):
            total = total + g_rs[side, o]
        g_ar[side, col] = total
        send_col(lambda o, peer: g_ar.at[side, col], lambda o: g_ar.at[side, col], g_ar_sem.at[side], send_sem.at[3 + side])

    def gram_ag_send(side):
        wait_bytes(g_ar.at[side, pl.ds(0, COLS - 1)], g_ar_sem.at[side])
        total = g_ar[side, 0]
        for c in range(1, COLS):
            total = total + g_ar[side, c]
        g_all[side, row] = total
        send_row(lambda o, peer: g_all.at[side, row], lambda o: g_all.at[side, row], g_ag_sem.at[side], send_sem.at[5 + side])

    def gram_wait(side):
        wait_bytes(g_all.at[side, pl.ds(0, ROWS - 1)], g_ag_sem.at[side])
        k = 0
        for i in range(3):
            for j in range(i + 1):
                for t in range(16):
                    at = 128 * k + 8 * t
                    weights[128 * i + 8 * t : 128 * i + 8 * t + 8, 128 * j : 128 * j + 128] = g_all[side, at // 24, at % 24 : at % 24 + 8, :] * (-1.0 / N / N)
                block = weights[128 * i : 128 * i + 128, 128 * j : 128 * j + 128]
                if i == j:
                    same = lanes_of((128, LANES)) == lax.broadcasted_iota(jnp.int32, (128, LANES), 0)
                    weights[128 * i : 128 * i + 128, 128 * j : 128 * j + 128] = block + jnp.where(same, 2.0 / N, 0.0)
                else:
                    weights[128 * j : 128 * j + 128, 128 * i : 128 * i + 128] = jnp.transpose(block)
                k += 1

    start_gram(0, left_set)

    lane16 = lanes_of((BLOCK, LANES))

    def joined(slots):
        chunks = []
        for group in range(2):
            first, second, third, fourth = (unpack(slots(4 * group + k).astype(F32), k) for k in range(4))
            chunks.append(jnp.where(lane16 < 96, first, second).astype(BF16))
            chunks.append(jnp.where(lane16 < 64, second, third).astype(BF16))
            chunks.append(jnp.where(lane16 < 32, third, fourth).astype(BF16))
        return jnp.concatenate(chunks, axis=1)

    def pieces(values):
        first, second, third = (values[:, 128 * k : 128 * k + 128] for k in range(3))
        turned_pieces = (first, jnp.where(lane16 < 64, second, first), jnp.where(lane16 < 64, third, second), third)
        return [pack(piece, k) for k, piece in enumerate(turned_pieces)]

    load_matrix.wait()
    for y in (0, 1, 3, 2):
        wait_bytes(b_slots.at[pl.ds(0, 7 if y == 0 else 8)], b_sem.at[y])
        source = lax.rem(plane + (4 - y), 4)
        b_all[...] = joined(lambda k: b_slots[8 * source + k])
        if y == 2:
            gram_rs_send(0)
        part = lax.dot_general(
            b_all[...], matrix[:, pl.ds(pl.multiple_of(768 * source, 768), 768)], (((1,), (1,)), ((), ())), preferred_element_type=F32
        )
        if y == 0:
            image_sum[...] = part
        else:
            image_sum[...] += part
    for half in range(2):
        for k, piece in enumerate(pieces(image_sum[:, 384 * half : 384 * half + 384])):
            image_send[4 * half + k] = piece
    send_col(lambda o, peer: image_send.at[peer], lambda o: image_recv.at[o - 1], image_sem, send_sem.at[7])
    start_gram(1, right_set)
    wait_bytes(image_recv, image_sem)
    valid_left = valid_lanes((BLOCK, LANES), q_left)
    valid_right = valid_lanes((BLOCK, LANES), q_right)
    image = image_send[col]
    for o in range(COLS - 1):
        image = image + image_recv[o]
    image = jnp.where(valid_left, unpack(image, q_left), 0.0)

    def sums_rs_send(side, values, basis):
        for i in range(3):
            p_local[side, 64 * i : 64 * i + 64, :] = dot_nt(values, basis[128 * i : 128 * i + 128, :])
        p_local[side, 192:256, 0:BLOCK] = dot_nt(values, values)
        p_local[side, 192:256, BLOCK:LANES] = jnp.zeros((BLOCK, LANES - BLOCK), F32)
        send_row(lambda o, peer: p_local.at[side, pl.ds(pl.multiple_of(8 * peer, 8), 8)], lambda o: p_rs.at[side, o - 1], p_rs_sem.at[side], send_sem.at[8 + side])

    def sums_ar_send(side):
        wait_bytes(p_rs.at[side], p_rs_sem.at[side])
        total = p_local[side, pl.ds(pl.multiple_of(8 * row, 8), 8), :]
        for o in range(ROWS - 1):
            total = total + p_rs[side, o]
        p_ar[side, col] = total
        send_col(lambda o, peer: p_ar.at[side, col], lambda o: p_ar.at[side, col], p_ar_sem.at[side], send_sem.at[10 + side])

    def sums_ag_send(side):
        wait_bytes(p_ar.at[side, pl.ds(0, COLS - 1)], p_ar_sem.at[side])
        total = p_ar[side, 0]
        for c in range(1, COLS):
            total = total + p_ar[side, c]
        p_all[side, row] = total
        send_row(lambda o, peer: p_all.at[side, row], lambda o: p_all.at[side, row], p_ag_sem.at[side], send_sem.at[12 + side])

    def sums_wait(side):
        wait_bytes(p_all.at[side, pl.ds(0, ROWS - 1)], p_ag_sem.at[side])

    def finish(side, values, basis):
        sums = [jnp.concatenate([p_all[side, 8 * i + t] for t in range(8)], axis=0) for i in range(4)]
        joint = jnp.concatenate(sums[0:3], axis=1)
        gram = sums[3][:, 0:BLOCK] - dot_nt(dot_nn(joint, weights[...]), joint)
        projected = values - dot_nn(joint * (1.0 / N), basis[...])
        eliminated = cholesky_and_inverse(gram * (1.0 / N))
        new_block = dot_nn(eliminated[:, BLOCK:LANES], projected)
        upper = jnp.where(lane16 >= lax.broadcasted_iota(jnp.int32, (BLOCK, LANES), 0), eliminated, 0.0)
        return new_block, upper

    def write_factor(side, upper):
        factors_out[side] = jnp.transpose(upper)[0:BLOCK, :]

    sums_rs_send(0, image, left_set)
    gram_ar_send(0)
    sums_ar_send(0)
    gram_ag_send(0)
    sums_ag_send(0)
    gram_wait(0)
    sums_wait(0)
    gram_rs_send(1)
    left_new, left_upper = finish(0, image, left_set)
    u_slots[col] = pack(left_new, q_left).astype(BF16)
    send_col(lambda o, peer: u_slots.at[col], lambda o: u_slots.at[col], u_sem, send_sem.at[14])
    gram_ar_send(1)
    left_out[...] = pltpu.roll(left_new, left_back, 1)[:, 0:WIDTH]
    write_factor(0, left_upper)

    wait_bytes(u_slots.at[pl.ds(0, COLS - 1)], u_sem)
    u_all[...] = joined(lambda k: u_slots[k])

    def send_piece(peer, y):
        pltpu.make_async_remote_copy(
            src_ref=co_send.at[peer], dst_ref=co_recv.at[8 * y + within], send_sem=send_sem.at[15], recv_sem=co_sem.at[y],
            device_id=(col, peer), device_id_type=MESH,
        ).start()

    for y in (2, 1, 3, 0):
        target = lax.rem(plane + y, 4)
        part = lax.dot_general(
            u_all[...], matrix[:, pl.ds(pl.multiple_of(768 * target, 768), 768)], (((1,), (0,)), ((), ())), preferred_element_type=F32
        )
        for half in range(2):
            for k, piece in enumerate(pieces(part[:, 384 * half : 384 * half + 384])):
                co_send[8 * target + 4 * half + k] = piece.astype(BF16)
        if y == 0:
            def send_piece_near(w, carry):
                send_piece(own_plane_peer(w), 0)
                return carry

            lax.fori_loop(1, 8, send_piece_near, 0)
        else:
            def send_piece_far(w, carry, y=y):
                send_piece(other_plane_peer(y, w), y)
                return carry

            lax.fori_loop(0, 8, send_piece_far, 0)
    co_recv[within] = co_send[row]
    coimage = jnp.zeros((48, LANES), F32)
    for y in (0, 1, 3, 2):
        wait_bytes(co_recv.at[pl.ds(8 * y, 7 if y == 0 else 8)], co_sem.at[y])
        for w in range(8):
            coimage = coimage + co_recv[8 * y + w].astype(F32)
    coimage = jnp.where(valid_right, unpack(coimage, q_right), 0.0)
    sums_rs_send(1, coimage, right_set)
    sums_ar_send(1)
    gram_ag_send(1)
    sums_ag_send(1)
    gram_wait(1)
    sums_wait(1)
    right_new, right_upper = finish(1, coimage, right_set)
    right_out[...] = pltpu.roll(right_new, right_back, 1)[:, 0:WIDTH]
    write_factor(1, right_upper)

    wait_bytes(b_slots.at[pl.ds(0, ROWS - 1)], send_sem.at[0])
    wait_bytes(image_recv, send_sem.at[7])
    wait_bytes(u_slots.at[pl.ds(0, COLS - 1)], send_sem.at[14])
    wait_bytes(co_recv.at[pl.ds(0, ROWS - 1)], send_sem.at[15])
    for side in range(2):
        wait_bytes(g_rs.at[side], send_sem.at[1 + side])
        wait_bytes(g_ar.at[side, pl.ds(0, COLS - 1)], send_sem.at[3 + side])
        wait_bytes(g_all.at[side, pl.ds(0, ROWS - 1)], send_sem.at[5 + side])
        wait_bytes(p_rs.at[side], send_sem.at[8 + side])
        wait_bytes(p_ar.at[side, pl.ds(0, COLS - 1)], send_sem.at[10 + side])
        wait_bytes(p_all.at[side, pl.ds(0, ROWS - 1)], send_sem.at[12 + side])


def shards(matrix, left_basis, right_basis, right_block):
    in_hbm = pl.BlockSpec(memory_space=pltpu.HBM)
    in_vmem = pl.BlockSpec(memory_space=pltpu.VMEM)
    dma = pltpu.SemaphoreType.DMA
    return pl.pallas_call(
        kernel,
        out_shape=(
            jax.ShapeDtypeStruct((BLOCK, WIDTH), F32),
            jax.ShapeDtypeStruct((BLOCK, WIDTH), F32),
            jax.ShapeDtypeStruct((2, BLOCK, BLOCK), F32),
        ),
        in_specs=[in_hbm] * 4,
        out_specs=(in_vmem, in_vmem, in_vmem),
        scratch_shapes=[
            pltpu.VMEM((768, 3072), BF16),
            pltpu.VMEM((WIDTH, PRIOR_ROWS), F32),
            pltpu.VMEM((WIDTH, PRIOR_ROWS), F32),
            pltpu.VMEM((BLOCK, WIDTH), F32),
            pltpu.VMEM((LANES, SET_ROWS), F32),
            pltpu.VMEM((SET_ROWS, LANES), F32),
            pltpu.VMEM((SET_ROWS, LANES), F32),
            pltpu.VMEM((ROWS, 48, LANES), BF16),
            pltpu.VMEM((BLOCK, 768), BF16),
            pltpu.VMEM((BLOCK, 768), F32),
            pltpu.VMEM((COLS, 48, LANES), F32),
            pltpu.VMEM((COLS - 1, 48, LANES), F32),
            pltpu.VMEM((COLS, 48, LANES), BF16),
            pltpu.VMEM((BLOCK, 768), BF16),
            pltpu.VMEM((ROWS, 48, LANES), BF16),
            pltpu.VMEM((ROWS, 48, LANES), BF16),
            pltpu.VMEM((2, 256, LANES), F32),
            pltpu.VMEM((2, ROWS - 1, 8, LANES), F32),
            pltpu.VMEM((2, COLS, 8, LANES), F32),
            pltpu.VMEM((2, ROWS, 8, LANES), F32),
            pltpu.VMEM((2, 768, LANES), F32),
            pltpu.VMEM((2, ROWS - 1, 24, LANES), F32),
            pltpu.VMEM((2, COLS, 24, LANES), F32),
            pltpu.VMEM((2, ROWS, 24, LANES), F32),
            pltpu.VMEM((SET_ROWS, SET_ROWS), F32),
            dma((4,)), dma((16,)), dma((4,)), dma(()), dma(()), dma((4,)),
            dma((2,)), dma((2,)), dma((2,)), dma((2,)), dma((2,)), dma((2,)),
        ],
        compiler_params=pltpu.CompilerParams(
            collective_id=0, has_side_effects=True, vmem_limit_bytes=(53 * 1024 + 768) * 1024
        ),
        cost_estimate=pl.CostEstimate(flops=700_000_000, bytes_accessed=8_000_000, transcendentals=0),
    )(matrix, left_basis.T, right_basis.T, right_block)


def solution(mesh):
    in_specs = (
        P("row", "col"),
        P(None, ("row", "col")),
        P(None, ("col", "row")),
        P(None, ("col", "row")),
    )
    out_specs = (P(None, ("row", "col")), P(None, ("col", "row")), P())
    return jax.shard_map(shards, mesh=mesh, in_specs=in_specs, out_specs=out_specs, check_vma=False)
```

```python
import jax
import jax.numpy as jnp
from jax import lax
from jax.experimental import pallas as pl
from jax.experimental.pallas import tpu as pltpu
from jax.sharding import PartitionSpec as P

N = 24576
BLOCK = 64
PRIOR_ROWS = 320
SET_ROWS = 384
COLS = 8
ROWS = 32
WIDTH = 96
LANES = 128
MESH = pl.DeviceIdType.MESH
F32 = jnp.float32
BF16 = jnp.bfloat16
highest_precision = lax.Precision.HIGHEST


def dot_nn(first, second):
    return lax.dot_general(first, second, (((1,), (0,)), ((), ())), precision=highest_precision, preferred_element_type=F32)


def dot_nt(first, second):
    return lax.dot_general(first, second, (((1,), (1,)), ((), ())), precision=highest_precision, preferred_element_type=F32)


def wait_bytes(ref, sem):
    pltpu.make_async_copy(ref, ref, sem).wait()


def lanes_of(shape):
    return lax.broadcasted_iota(jnp.int32, shape, 1)


def valid_lanes(shape, q):
    return lax.rem(lanes_of(shape) + 32 * q, LANES) < WIDTH


def pack(values, q):
    moved = jnp.concatenate([pltpu.roll(values[48:64, :], 32 * (3 - k), 1) for k in range(3)], axis=0)
    return jnp.where(valid_lanes((48, LANES), q), values[0:48, :], moved)


def unpack(packed, q):
    group = lax.rem(lanes_of((16, LANES)) + 32 * q, LANES)
    back = [pltpu.roll(packed[16 * k : 16 * k + 16, :], 32 * (1 + k), 1) for k in range(3)]
    last = jnp.where(group < 32, back[0], jnp.where(group < 64, back[1], back[2]))
    return jnp.concatenate([packed, last], axis=0)


def cholesky_and_inverse(gram):
    lane = lanes_of((8, LANES))
    sub = lax.broadcasted_iota(jnp.int32, (8, LANES), 0)

    def spread(values):
        return jnp.broadcast_to(values, (8, LANES))

    blocks = []
    for k in range(8):
        unit = jnp.where(lane == sub + (BLOCK + 8 * k), 1.0, 0.0)
        padded = jnp.concatenate([gram[8 * k : 8 * k + 8, :], jnp.zeros((8, BLOCK), F32)], axis=1)
        blocks.append(padded + unit)
    for b in range(8):
        columns = [[spread(blocks[k][:, 8 * b + i : 8 * b + i + 1]) for k in range(b, 8)] for i in range(8)]
        for i in range(8):
            inverse = lax.rsqrt(spread(columns[i][0][i : i + 1, :]))
            lower = [column * inverse for column in columns[i]]
            row = spread(blocks[b][i : i + 1, :]) * inverse
            for m in range(i + 1, 8):
                weight = spread(lower[0][m : m + 1, :])
                columns[m] = [column - below * weight for column, below in zip(columns[m], lower)]
            updated = blocks[b] - lower[0] * row
            blocks[b] = jnp.where(sub > i, updated, jnp.where(sub == i, row, blocks[b]))
            for k in range(b + 1, 8):
                blocks[k] = blocks[k] - lower[k - b] * row
    return jnp.concatenate(blocks, axis=0)


def kernel(
    matrix_hbm, left_hbm, right_hbm, block_hbm,
    left_out, right_out, factors_out,
    matrix, left_in, right_in, block_in,
    turned, left_set, right_set,
    b_slots, b_all, image_sum, image_send, image_recv,
    u_slots, u_all, pair_send, pair_recv, co_send, co_recv,
    p_local, p_rs, p_ar, p_all,
    g_local, g_rs, g_ar, g_all, weights,
    load_sem, send_sem, b_sem, pass_sem, image_sem, u_sem, pair_sem, co_sem,
    p_rs_sem, p_ar_sem, p_ag_sem, g_rs_sem, g_ar_sem, g_ag_sem,
):
    col = lax.axis_index("col")
    row = lax.axis_index("row")
    q_left = lax.rem(col, 4)
    q_right = lax.rem(row, 4)

    def row_peer(o):
        return lax.rem(row + o, ROWS)

    def col_peer(o):
        return lax.rem(col + o, COLS)

    barrier = pltpu.get_barrier_semaphore()

    def greet_row(o, carry):
        pl.semaphore_signal(barrier, inc=1, device_id=(col, row_peer(o)), device_id_type=MESH)
        return carry

    def greet_col(o, carry):
        pl.semaphore_signal(barrier, inc=1, device_id=(col_peer(o), row), device_id_type=MESH)
        return carry

    load_block = pltpu.make_async_copy(block_hbm, block_in, load_sem.at[0])
    load_left = pltpu.make_async_copy(left_hbm, left_in, load_sem.at[1])
    load_right = pltpu.make_async_copy(right_hbm, right_in, load_sem.at[2])
    load_matrix = pltpu.make_async_copy(matrix_hbm, matrix, load_sem.at[3])
    load_block.start()
    lax.fori_loop(1, ROWS, greet_row, 0)
    lax.fori_loop(1, COLS, greet_col, 0)
    load_left.start()
    load_right.start()
    load_matrix.start()

    def send_row(source, target, sem, send):
        def body(k, carry):
            o = lax.rem(k + 15, ROWS - 1) + 1
            peer = row_peer(o)
            pltpu.make_async_remote_copy(
                src_ref=source(o, peer), dst_ref=target(o), send_sem=send, recv_sem=sem,
                device_id=(col, peer), device_id_type=MESH,
            ).start()
            return carry

        lax.fori_loop(0, ROWS - 1, body, 0)

    def send_col(source, target, sem, send):
        def body(k, carry):
            o = lax.rem(k + 3, COLS - 1) + 1
            peer = col_peer(o)
            pltpu.make_async_remote_copy(
                src_ref=source(o, peer), dst_ref=target(o), send_sem=send, recv_sem=sem,
                device_id=(peer, row), device_id_type=MESH,
            ).start()
            return carry

        lax.fori_loop(0, COLS - 1, body, 0)

    right_shift = lax.rem(96 * q_right, LANES)
    right_back = lax.rem(32 * q_right, LANES)
    left_back = lax.rem(32 * q_left, LANES)

    turned[...] = jnp.zeros_like(turned)
    load_block.wait()
    left_set[0:BLOCK, :] = jnp.zeros((BLOCK, LANES), F32)
    left_set[0:BLOCK, 0:WIDTH] = block_in[...]
    turned_block = pltpu.roll(left_set[0:BLOCK, :], right_shift, 1)
    plane, across, core = row // 8, lax.rem(row, 8) // 2, lax.rem(row, 2)
    sibling = row + 1 - 2 * core
    own_slot = 8 * plane + 4 * core + across
    b_slots[own_slot] = pack(turned_block, q_right).astype(BF16)
    pl.semaphore_wait(barrier, ROWS + COLS - 2)

    def chip_peer(y, x):
        return 8 * lax.rem(plane + y, 4) + 2 * x + core

    def to_plane(y, send):
        def near(w, carry):
            x = lax.rem(across + w, 4)
            send(chip_peer(y, x), x)
            return carry

        lax.fori_loop(1 if y == 0 else 0, 4, near, 0)

    for y in (0, 1, 3, 2):

        def send_block(peer, x, y=y):
            pltpu.make_async_remote_copy(
                src_ref=b_slots.at[own_slot], dst_ref=b_slots.at[own_slot], send_sem=send_sem.at[0], recv_sem=b_sem.at[y],
                device_id=(col, peer), device_id_type=MESH,
            ).start()

        to_plane(y, send_block)

    def turn(basis, q, out):
        for k in range(3):
            place = pl.multiple_of(32 * lax.rem(k + 3 * q, 4), 32)
            turned[pl.ds(place, 32), 0:PRIOR_ROWS] = basis[32 * k : 32 * k + 32, :]
        turned[pl.ds(pl.multiple_of(32 * lax.rem(3 + 3 * q, 4), 32), 32), :] = jnp.zeros((32, SET_ROWS), F32)
        for i in range(3):
            out[128 * i : 128 * i + 128, :] = jnp.transpose(turned[:, 128 * i : 128 * i + 128])

    load_left.wait()
    turn(left_in, q_left, left_set)
    load_right.wait()
    turn(right_in, q_right, right_set)
    right_set[PRIOR_ROWS:SET_ROWS, :] = turned_block

    def start_gram(side, basis):
        k = 0
        for i in range(3):
            for j in range(i + 1):
                block = dot_nt(basis[128 * i : 128 * i + 128, :], basis[128 * j : 128 * j + 128, :])
                g_local[side, 128 * k : 128 * k + 128, :] = block
                k += 1

    def gram_rs_send(side):
        send_row(lambda o, peer: g_local.at[side, pl.ds(pl.multiple_of(24 * peer, 8), 24)], lambda o: g_rs.at[side, o - 1], g_rs_sem.at[side], send_sem.at[1 + side])

    def gram_ar_send(side):
        wait_bytes(g_rs.at[side], g_rs_sem.at[side])
        total = g_local[side, pl.ds(pl.multiple_of(24 * row, 8), 24), :]
        for o in range(ROWS - 1):
            total = total + g_rs[side, o]
        g_ar[side, col] = total
        send_col(lambda o, peer: g_ar.at[side, col], lambda o: g_ar.at[side, col], g_ar_sem.at[side], send_sem.at[3 + side])

    def gram_ag_send(side):
        wait_bytes(g_ar.at[side, pl.ds(0, COLS - 1)], g_ar_sem.at[side])
        total = g_ar[side, 0]
        for c in range(1, COLS):
            total = total + g_ar[side, c]
        g_all[side, row] = total
        send_row(lambda o, peer: g_all.at[side, row], lambda o: g_all.at[side, row], g_ag_sem.at[side], send_sem.at[5 + side])

    def gram_wait(side):
        wait_bytes(g_all.at[side, pl.ds(0, ROWS - 1)], g_ag_sem.at[side])
        k = 0
        for i in range(3):
            for j in range(i + 1):
                for t in range(16):
                    at = 128 * k + 8 * t
                    weights[128 * i + 8 * t : 128 * i + 8 * t + 8, 128 * j : 128 * j + 128] = g_all[side, at // 24, at % 24 : at % 24 + 8, :] * (-1.0 / N / N)
                block = weights[128 * i : 128 * i + 128, 128 * j : 128 * j + 128]
                if i == j:
                    same = lanes_of((128, LANES)) == lax.broadcasted_iota(jnp.int32, (128, LANES), 0)
                    weights[128 * i : 128 * i + 128, 128 * j : 128 * j + 128] = block + jnp.where(same, 2.0 / N, 0.0)
                else:
                    weights[128 * j : 128 * j + 128, 128 * i : 128 * i + 128] = jnp.transpose(block)
                k += 1

    start_gram(0, left_set)

    lane16 = lanes_of((BLOCK, LANES))

    def joined(slots):
        chunks = []
        for group in range(2):
            first, second, third, fourth = (unpack(slots(4 * group + k).astype(F32), k) for k in range(4))
            chunks.append(jnp.where(lane16 < 96, first, second).astype(BF16))
            chunks.append(jnp.where(lane16 < 64, second, third).astype(BF16))
            chunks.append(jnp.where(lane16 < 32, third, fourth).astype(BF16))
        return jnp.concatenate(chunks, axis=1)

    def pieces(values):
        first, second, third = (values[:, 128 * k : 128 * k + 128] for k in range(3))
        turned_pieces = (first, jnp.where(lane16 < 64, second, first), jnp.where(lane16 < 64, third, second), third)
        return [pack(piece, k) for k, piece in enumerate(turned_pieces)]

    load_matrix.wait()
    def pass_to_sibling(y):
        wait_bytes(b_slots.at[pl.ds(0, 3 if y == 0 else 4)], b_sem.at[y])
        own = b_slots.at[pl.ds(8 * lax.rem(plane + (4 - y), 4) + 4 * core, 4)]
        pltpu.make_async_remote_copy(
            src_ref=own, dst_ref=own, send_sem=send_sem.at[16], recv_sem=pass_sem.at[y],
            device_id=(col, sibling), device_id_type=MESH,
        ).start()

    def multiply(y):
        wait_bytes(b_slots.at[pl.ds(0, 4)], pass_sem.at[y])
        source = lax.rem(plane + (4 - y), 4)
        b_all[...] = joined(lambda k: b_slots[8 * source + 4 * (k % 2) + k // 2])
        part = lax.dot_general(
            b_all[...], matrix[:, pl.ds(pl.multiple_of(768 * source, 768), 768)], (((1,), (1,)), ((), ())), preferred_element_type=F32
        )
        if y == 0:
            image_sum[...] = part
        else:
            image_sum[...] += part

    pass_to_sibling(0)
    pass_to_sibling(1)
    multiply(0)
    pass_to_sibling(3)
    multiply(1)
    pass_to_sibling(2)
    multiply(3)
    multiply(2)
    for half in range(2):
        for k, piece in enumerate(pieces(image_sum[:, 384 * half : 384 * half + 384])):
            image_send[4 * half + k] = piece
    send_col(lambda o, peer: image_send.at[peer], lambda o: image_recv.at[o - 1], image_sem, send_sem.at[7])
    gram_rs_send(0)
    start_gram(1, right_set)
    wait_bytes(image_recv, image_sem)
    valid_left = valid_lanes((BLOCK, LANES), q_left)
    valid_right = valid_lanes((BLOCK, LANES), q_right)
    image = image_send[col]
    for o in range(COLS - 1):
        image = image + image_recv[o]
    image = jnp.where(valid_left, unpack(image, q_left), 0.0)

    def sums_rs_send(side, values, basis):
        for i in range(3):
            p_local[side, 64 * i : 64 * i + 64, :] = dot_nt(values, basis[128 * i : 128 * i + 128, :])
        p_local[side, 192:256, 0:BLOCK] = dot_nt(values, values)
        p_local[side, 192:256, BLOCK:LANES] = jnp.zeros((BLOCK, LANES - BLOCK), F32)
        send_row(lambda o, peer: p_local.at[side, pl.ds(pl.multiple_of(8 * peer, 8), 8)], lambda o: p_rs.at[side, o - 1], p_rs_sem.at[side], send_sem.at[8 + side])

    def sums_ar_send(side):
        wait_bytes(p_rs.at[side], p_rs_sem.at[side])
        total = p_local[side, pl.ds(pl.multiple_of(8 * row, 8), 8), :]
        for o in range(ROWS - 1):
            total = total + p_rs[side, o]
        p_ar[side, col] = total
        send_col(lambda o, peer: p_ar.at[side, col], lambda o: p_ar.at[side, col], p_ar_sem.at[side], send_sem.at[10 + side])

    def sums_ag_send(side):
        wait_bytes(p_ar.at[side, pl.ds(0, COLS - 1)], p_ar_sem.at[side])
        total = p_ar[side, 0]
        for c in range(1, COLS):
            total = total + p_ar[side, c]
        p_all[side, row] = total
        send_row(lambda o, peer: p_all.at[side, row], lambda o: p_all.at[side, row], p_ag_sem.at[side], send_sem.at[12 + side])

    def sums_wait(side):
        wait_bytes(p_all.at[side, pl.ds(0, ROWS - 1)], p_ag_sem.at[side])

    def finish(side, values, basis):
        sums = [jnp.concatenate([p_all[side, 8 * i + t] for t in range(8)], axis=0) for i in range(4)]
        joint = jnp.concatenate(sums[0:3], axis=1)
        gram = sums[3][:, 0:BLOCK] - dot_nt(dot_nn(joint, weights[...]), joint)
        projected = values - dot_nn(joint * (1.0 / N), basis[...])
        eliminated = cholesky_and_inverse(gram * (1.0 / N))
        new_block = dot_nn(eliminated[:, BLOCK:LANES], projected)
        upper = jnp.where(lane16 >= lax.broadcasted_iota(jnp.int32, (BLOCK, LANES), 0), eliminated, 0.0)
        return new_block, upper

    def write_factor(side, upper):
        factors_out[side] = jnp.transpose(upper)[0:BLOCK, :]

    sums_rs_send(0, image, left_set)
    gram_ar_send(0)
    sums_ar_send(0)
    gram_ag_send(0)
    sums_ag_send(0)
    gram_wait(0)
    sums_wait(0)
    left_new, left_upper = finish(0, image, left_set)
    u_slots[col] = pack(left_new, q_left).astype(BF16)
    send_col(lambda o, peer: u_slots.at[col], lambda o: u_slots.at[col], u_sem, send_sem.at[14])
    gram_rs_send(1)
    left_out[...] = pltpu.roll(left_new, left_back, 1)[:, 0:WIDTH]
    write_factor(0, left_upper)

    wait_bytes(u_slots.at[pl.ds(0, COLS - 1)], u_sem)
    u_all[...] = joined(lambda k: u_slots[k])

    def multiply_back(y):
        target = lax.rem(plane + y, 4)
        part = lax.dot_general(
            u_all[...], matrix[:, pl.ds(pl.multiple_of(768 * target, 768), 768)], (((1,), (0,)), ((), ())), preferred_element_type=F32
        )
        for half in range(2):
            for k, piece in enumerate(pieces(part[:, 384 * half : 384 * half + 384])):
                pair_send[y, k % 2, 2 * half + k // 2] = piece
        pltpu.make_async_remote_copy(
            src_ref=pair_send.at[y, 1 - core], dst_ref=pair_recv.at[y], send_sem=send_sem.at[17], recv_sem=pair_sem.at[y],
            device_id=(col, sibling), device_id_type=MESH,
        ).start()

    def send_pieces(y):
        wait_bytes(pair_recv.at[y], pair_sem.at[y])
        for x in range(4):
            co_send[y, x] = (pair_send[y, core, x] + pair_recv[y, x]).astype(BF16)

        def send_piece(peer, x):
            pltpu.make_async_remote_copy(
                src_ref=co_send.at[y, x], dst_ref=co_recv.at[y, across], send_sem=send_sem.at[15], recv_sem=co_sem.at[y],
                device_id=(col, peer), device_id_type=MESH,
            ).start()

        to_plane(y, send_piece)

    multiply_back(2)
    multiply_back(1)
    send_pieces(2)
    multiply_back(3)
    send_pieces(1)
    multiply_back(0)
    send_pieces(3)
    send_pieces(0)
    co_recv[0, across] = co_send[0, across]
    gram_ar_send(1)
    coimage = jnp.zeros((48, LANES), F32)
    for y in (0, 1, 3, 2):
        wait_bytes(co_recv.at[y, pl.ds(0, 3 if y == 0 else 4)], co_sem.at[y])
        for x in range(4):
            coimage = coimage + co_recv[y, x].astype(F32)
    coimage = jnp.where(valid_right, unpack(coimage, q_right), 0.0)
    sums_rs_send(1, coimage, right_set)
    sums_ar_send(1)
    gram_ag_send(1)
    sums_ag_send(1)
    gram_wait(1)
    sums_wait(1)
    right_new, right_upper = finish(1, coimage, right_set)
    right_out[...] = pltpu.roll(right_new, right_back, 1)[:, 0:WIDTH]
    write_factor(1, right_upper)

    wait_bytes(b_slots.at[pl.ds(0, 15)], send_sem.at[0])
    wait_bytes(b_slots.at[pl.ds(0, 16)], send_sem.at[16])
    wait_bytes(image_recv, send_sem.at[7])
    wait_bytes(u_slots.at[pl.ds(0, COLS - 1)], send_sem.at[14])
    for y in range(4):
        wait_bytes(co_recv.at[y, pl.ds(0, 3 if y == 0 else 4)], send_sem.at[15])
        wait_bytes(pair_recv.at[y], send_sem.at[17])
    for side in range(2):
        wait_bytes(g_rs.at[side], send_sem.at[1 + side])
        wait_bytes(g_ar.at[side, pl.ds(0, COLS - 1)], send_sem.at[3 + side])
        wait_bytes(g_all.at[side, pl.ds(0, ROWS - 1)], send_sem.at[5 + side])
        wait_bytes(p_rs.at[side], send_sem.at[8 + side])
        wait_bytes(p_ar.at[side, pl.ds(0, COLS - 1)], send_sem.at[10 + side])
        wait_bytes(p_all.at[side, pl.ds(0, ROWS - 1)], send_sem.at[12 + side])


def shards(matrix, left_basis, right_basis, right_block):
    in_hbm = pl.BlockSpec(memory_space=pltpu.HBM)
    in_vmem = pl.BlockSpec(memory_space=pltpu.VMEM)
    dma = pltpu.SemaphoreType.DMA
    return pl.pallas_call(
        kernel,
        out_shape=(
            jax.ShapeDtypeStruct((BLOCK, WIDTH), F32),
            jax.ShapeDtypeStruct((BLOCK, WIDTH), F32),
            jax.ShapeDtypeStruct((2, BLOCK, BLOCK), F32),
        ),
        in_specs=[in_hbm] * 4,
        out_specs=(in_vmem, in_vmem, in_vmem),
        scratch_shapes=[
            pltpu.VMEM((768, 3072), BF16),
            pltpu.VMEM((WIDTH, PRIOR_ROWS), F32),
            pltpu.VMEM((WIDTH, PRIOR_ROWS), F32),
            pltpu.VMEM((BLOCK, WIDTH), F32),
            pltpu.VMEM((LANES, SET_ROWS), F32),
            pltpu.VMEM((SET_ROWS, LANES), F32),
            pltpu.VMEM((SET_ROWS, LANES), F32),
            pltpu.VMEM((ROWS, 48, LANES), BF16),
            pltpu.VMEM((BLOCK, 768), BF16),
            pltpu.VMEM((BLOCK, 768), F32),
            pltpu.VMEM((COLS, 48, LANES), F32),
            pltpu.VMEM((COLS - 1, 48, LANES), F32),
            pltpu.VMEM((COLS, 48, LANES), BF16),
            pltpu.VMEM((BLOCK, 768), BF16),
            pltpu.VMEM((4, 2, 4, 48, LANES), F32),
            pltpu.VMEM((4, 4, 48, LANES), F32),
            pltpu.VMEM((4, 4, 48, LANES), BF16),
            pltpu.VMEM((4, 4, 48, LANES), BF16),
            pltpu.VMEM((2, 256, LANES), F32),
            pltpu.VMEM((2, ROWS - 1, 8, LANES), F32),
            pltpu.VMEM((2, COLS, 8, LANES), F32),
            pltpu.VMEM((2, ROWS, 8, LANES), F32),
            pltpu.VMEM((2, 768, LANES), F32),
            pltpu.VMEM((2, ROWS - 1, 24, LANES), F32),
            pltpu.VMEM((2, COLS, 24, LANES), F32),
            pltpu.VMEM((2, ROWS, 24, LANES), F32),
            pltpu.VMEM((SET_ROWS, SET_ROWS), F32),
            dma((4,)), dma((18,)), dma((4,)), dma((4,)), dma(()), dma(()), dma((4,)), dma((4,)),
            dma((2,)), dma((2,)), dma((2,)), dma((2,)), dma((2,)), dma((2,)),
        ],
        compiler_params=pltpu.CompilerParams(
            collective_id=0, has_side_effects=True, vmem_limit_bytes=(53 * 1024 + 768) * 1024
        ),
        cost_estimate=pl.CostEstimate(flops=700_000_000, bytes_accessed=8_000_000, transcendentals=0),
    )(matrix, left_basis.T, right_basis.T, right_block)


def solution(mesh):
    in_specs = (
        P("row", "col"),
        P(None, ("row", "col")),
        P(None, ("col", "row")),
        P(None, ("col", "row")),
    )
    out_specs = (P(None, ("row", "col")), P(None, ("col", "row")), P())
    return jax.shard_map(shards, mesh=mesh, in_specs=in_specs, out_specs=out_specs, check_vma=False)
```

```python
import jax
import jax.numpy as jnp
from jax import lax
from jax.experimental import pallas as pl
from jax.experimental.pallas import tpu as pltpu
from jax.sharding import PartitionSpec as P

N = 24576
BLOCK = 64
PRIOR_ROWS = 320
SET_ROWS = 384
COLS = 8
ROWS = 32
WIDTH = 96
LANES = 128
MESH = pl.DeviceIdType.MESH
F32 = jnp.float32
BF16 = jnp.bfloat16
highest_precision = lax.Precision.HIGHEST


def dot_nn(first, second):
    return lax.dot_general(first, second, (((1,), (0,)), ((), ())), precision=highest_precision, preferred_element_type=F32)


def dot_nt(first, second):
    return lax.dot_general(first, second, (((1,), (1,)), ((), ())), precision=highest_precision, preferred_element_type=F32)


def wait_bytes(ref, sem):
    pltpu.make_async_copy(ref, ref, sem).wait()


def lanes_of(shape):
    return lax.broadcasted_iota(jnp.int32, shape, 1)


def valid_lanes(shape, q):
    return lax.rem(lanes_of(shape) + 32 * q, LANES) < WIDTH


def pack(values, q):
    moved = jnp.concatenate([pltpu.roll(values[48:64, :], 32 * (3 - k), 1) for k in range(3)], axis=0)
    return jnp.where(valid_lanes((48, LANES), q), values[0:48, :], moved)


def unpack(packed, q):
    group = lax.rem(lanes_of((16, LANES)) + 32 * q, LANES)
    back = [pltpu.roll(packed[16 * k : 16 * k + 16, :], 32 * (1 + k), 1) for k in range(3)]
    last = jnp.where(group < 32, back[0], jnp.where(group < 64, back[1], back[2]))
    return jnp.concatenate([packed, last], axis=0)


def cholesky_and_inverse(gram):
    lane = lanes_of((8, LANES))
    sub = lax.broadcasted_iota(jnp.int32, (8, LANES), 0)

    def spread(values):
        return jnp.broadcast_to(values, (8, LANES))

    blocks = []
    for k in range(8):
        unit = jnp.where(lane == sub + (BLOCK + 8 * k), 1.0, 0.0)
        padded = jnp.concatenate([gram[8 * k : 8 * k + 8, :], jnp.zeros((8, BLOCK), F32)], axis=1)
        blocks.append(padded + unit)
    for b in range(8):
        columns = [[spread(blocks[k][:, 8 * b + i : 8 * b + i + 1]) for k in range(b, 8)] for i in range(8)]
        for i in range(8):
            inverse = lax.rsqrt(spread(columns[i][0][i : i + 1, :]))
            lower = [column * inverse for column in columns[i]]
            row = spread(blocks[b][i : i + 1, :]) * inverse
            for m in range(i + 1, 8):
                weight = spread(lower[0][m : m + 1, :])
                columns[m] = [column - below * weight for column, below in zip(columns[m], lower)]
            updated = blocks[b] - lower[0] * row
            blocks[b] = jnp.where(sub > i, updated, jnp.where(sub == i, row, blocks[b]))
            for k in range(b + 1, 8):
                blocks[k] = blocks[k] - lower[k - b] * row
    return jnp.concatenate(blocks, axis=0)


def kernel(
    matrix_hbm, left_hbm, right_hbm, block_hbm,
    found_out,
    matrix, left_in, right_in, block_in,
    turned, left_set, right_set,
    b_slots, b_all, image_sum, image_send, image_recv,
    u_slots, u_all, pair_send, pair_recv, co_send, co_recv,
    p_local, p_rs, p_ar, p_all,
    g_local, g_rs, g_ar, g_all, weights,
    load_sem, send_sem, b_sem, pass_sem, image_sem, u_sem, pair_sem, co_sem,
    p_rs_sem, p_ar_sem, p_ag_sem, g_rs_sem, g_ar_sem, g_ag_sem,
):
    col = lax.axis_index("col")
    row = lax.axis_index("row")
    q_left = lax.rem(col, 4)
    q_right = lax.rem(row, 4)

    def row_peer(o):
        return lax.rem(row + o, ROWS)

    def col_peer(o):
        return lax.rem(col + o, COLS)

    barrier = pltpu.get_barrier_semaphore()

    def greet_row(o, carry):
        pl.semaphore_signal(barrier, inc=1, device_id=(col, row_peer(o)), device_id_type=MESH)
        return carry

    def greet_col(o, carry):
        pl.semaphore_signal(barrier, inc=1, device_id=(col_peer(o), row), device_id_type=MESH)
        return carry

    load_block = pltpu.make_async_copy(block_hbm, block_in, load_sem.at[0])
    load_left = pltpu.make_async_copy(left_hbm, left_in, load_sem.at[1])
    load_right = pltpu.make_async_copy(right_hbm, right_in, load_sem.at[2])
    load_matrix = pltpu.make_async_copy(matrix_hbm, matrix, load_sem.at[3])
    load_block.start()
    lax.fori_loop(1, ROWS, greet_row, 0)
    lax.fori_loop(1, COLS, greet_col, 0)
    load_left.start()
    load_right.start()
    load_matrix.start()

    def send_row(source, target, sem, send):
        def body(k, carry):
            o = lax.rem(k + 15, ROWS - 1) + 1
            peer = row_peer(o)
            pltpu.make_async_remote_copy(
                src_ref=source(o, peer), dst_ref=target(o), send_sem=send, recv_sem=sem,
                device_id=(col, peer), device_id_type=MESH,
            ).start()
            return carry

        lax.fori_loop(0, ROWS - 1, body, 0)

    def send_col(source, target, sem, send):
        def body(k, carry):
            o = lax.rem(k + 3, COLS - 1) + 1
            peer = col_peer(o)
            pltpu.make_async_remote_copy(
                src_ref=source(o, peer), dst_ref=target(o), send_sem=send, recv_sem=sem,
                device_id=(peer, row), device_id_type=MESH,
            ).start()
            return carry

        lax.fori_loop(0, COLS - 1, body, 0)

    right_shift = lax.rem(96 * q_right, LANES)
    right_back = lax.rem(32 * q_right, LANES)
    left_back = lax.rem(32 * q_left, LANES)

    turned[...] = jnp.zeros_like(turned)
    load_block.wait()
    left_set[0:BLOCK, :] = jnp.zeros((BLOCK, LANES), F32)
    left_set[0:BLOCK, 0:WIDTH] = block_in[...]
    turned_block = pltpu.roll(left_set[0:BLOCK, :], right_shift, 1)
    plane, across, core = row // 8, lax.rem(row, 8) // 2, lax.rem(row, 2)
    sibling = row + 1 - 2 * core
    own_slot = 8 * plane + 4 * core + across
    b_slots[own_slot] = pack(turned_block, q_right).astype(BF16)
    pl.semaphore_wait(barrier, ROWS + COLS - 2)

    def chip_peer(y, x):
        return 8 * lax.rem(plane + y, 4) + 2 * x + core

    def to_plane(y, send):
        def near(w, carry):
            x = lax.rem(across + w, 4)
            send(chip_peer(y, x), x)
            return carry

        lax.fori_loop(1 if y == 0 else 0, 4, near, 0)

    for y in (0, 1, 3, 2):

        def send_block(peer, x, y=y):
            pltpu.make_async_remote_copy(
                src_ref=b_slots.at[own_slot], dst_ref=b_slots.at[own_slot], send_sem=send_sem.at[0], recv_sem=b_sem.at[y],
                device_id=(col, peer), device_id_type=MESH,
            ).start()

        to_plane(y, send_block)

    def turn(basis, q, out):
        for k in range(3):
            place = pl.multiple_of(32 * lax.rem(k + 3 * q, 4), 32)
            turned[pl.ds(place, 32), 0:PRIOR_ROWS] = basis[32 * k : 32 * k + 32, :]
        turned[pl.ds(pl.multiple_of(32 * lax.rem(3 + 3 * q, 4), 32), 32), :] = jnp.zeros((32, SET_ROWS), F32)
        for i in range(3):
            out[128 * i : 128 * i + 128, :] = jnp.transpose(turned[:, 128 * i : 128 * i + 128])

    load_left.wait()
    turn(left_in, q_left, left_set)
    load_right.wait()
    turn(right_in, q_right, right_set)
    right_set[PRIOR_ROWS:SET_ROWS, :] = turned_block

    def start_gram(side, basis):
        k = 0
        for i in range(3):
            for j in range(i + 1):
                block = dot_nt(basis[128 * i : 128 * i + 128, :], basis[128 * j : 128 * j + 128, :])
                g_local[side, 128 * k : 128 * k + 128, :] = block
                k += 1

    def gram_rs_send(side):
        send_row(lambda o, peer: g_local.at[side, pl.ds(pl.multiple_of(24 * peer, 8), 24)], lambda o: g_rs.at[side, o - 1], g_rs_sem.at[side], send_sem.at[1 + side])

    def gram_ar_send(side):
        wait_bytes(g_rs.at[side], g_rs_sem.at[side])
        total = g_local[side, pl.ds(pl.multiple_of(24 * row, 8), 24), :]
        for o in range(ROWS - 1):
            total = total + g_rs[side, o]
        g_ar[side, col] = total
        send_col(lambda o, peer: g_ar.at[side, col], lambda o: g_ar.at[side, col], g_ar_sem.at[side], send_sem.at[3 + side])

    def gram_ag_send(side):
        wait_bytes(g_ar.at[side, pl.ds(0, COLS - 1)], g_ar_sem.at[side])
        total = g_ar[side, 0]
        for c in range(1, COLS):
            total = total + g_ar[side, c]
        g_all[side, row] = total
        send_row(lambda o, peer: g_all.at[side, row], lambda o: g_all.at[side, row], g_ag_sem.at[side], send_sem.at[5 + side])

    def gram_wait(side):
        wait_bytes(g_all.at[side, pl.ds(0, ROWS - 1)], g_ag_sem.at[side])
        k = 0
        for i in range(3):
            for j in range(i + 1):
                for t in range(16):
                    at = 128 * k + 8 * t
                    weights[128 * i + 8 * t : 128 * i + 8 * t + 8, 128 * j : 128 * j + 128] = g_all[side, at // 24, at % 24 : at % 24 + 8, :] * (-1.0 / N / N)
                block = weights[128 * i : 128 * i + 128, 128 * j : 128 * j + 128]
                if i == j:
                    same = lanes_of((128, LANES)) == lax.broadcasted_iota(jnp.int32, (128, LANES), 0)
                    weights[128 * i : 128 * i + 128, 128 * j : 128 * j + 128] = block + jnp.where(same, 2.0 / N, 0.0)
                else:
                    weights[128 * j : 128 * j + 128, 128 * i : 128 * i + 128] = jnp.transpose(block)
                k += 1

    start_gram(0, left_set)

    lane16 = lanes_of((BLOCK, LANES))

    def joined(slots):
        chunks = []
        for group in range(2):
            first, second, third, fourth = (unpack(slots(4 * group + k).astype(F32), k) for k in range(4))
            chunks.append(jnp.where(lane16 < 96, first, second).astype(BF16))
            chunks.append(jnp.where(lane16 < 64, second, third).astype(BF16))
            chunks.append(jnp.where(lane16 < 32, third, fourth).astype(BF16))
        return jnp.concatenate(chunks, axis=1)

    def pieces(values):
        first, second, third = (values[:, 128 * k : 128 * k + 128] for k in range(3))
        turned_pieces = (first, jnp.where(lane16 < 64, second, first), jnp.where(lane16 < 64, third, second), third)
        return [pack(piece, k) for k, piece in enumerate(turned_pieces)]

    load_matrix.wait()
    def pass_to_sibling(y):
        wait_bytes(b_slots.at[pl.ds(0, 3 if y == 0 else 4)], b_sem.at[y])
        own = b_slots.at[pl.ds(8 * lax.rem(plane + (4 - y), 4) + 4 * core, 4)]
        pltpu.make_async_remote_copy(
            src_ref=own, dst_ref=own, send_sem=send_sem.at[16], recv_sem=pass_sem.at[y],
            device_id=(col, sibling), device_id_type=MESH,
        ).start()

    def multiply(y):
        wait_bytes(b_slots.at[pl.ds(0, 4)], pass_sem.at[y])
        source = lax.rem(plane + (4 - y), 4)
        b_all[...] = joined(lambda k: b_slots[8 * source + 4 * (k % 2) + k // 2])
        part = lax.dot_general(
            b_all[...], matrix[:, pl.ds(pl.multiple_of(768 * source, 768), 768)], (((1,), (1,)), ((), ())), preferred_element_type=F32
        )
        if y == 0:
            image_sum[...] = part
        else:
            image_sum[...] += part

    pass_to_sibling(0)
    pass_to_sibling(1)
    multiply(0)
    pass_to_sibling(3)
    multiply(1)
    pass_to_sibling(2)
    multiply(3)
    multiply(2)
    for half in range(2):
        for k, piece in enumerate(pieces(image_sum[:, 384 * half : 384 * half + 384])):
            image_send[4 * half + k] = piece
    send_col(lambda o, peer: image_send.at[peer], lambda o: image_recv.at[o - 1], image_sem, send_sem.at[7])
    gram_rs_send(0)
    start_gram(1, right_set)
    wait_bytes(image_recv, image_sem)
    valid_left = valid_lanes((BLOCK, LANES), q_left)
    valid_right = valid_lanes((BLOCK, LANES), q_right)
    image = image_send[col]
    for o in range(COLS - 1):
        image = image + image_recv[o]
    image = jnp.where(valid_left, unpack(image, q_left), 0.0)

    def sums_rs_send(side, values, basis):
        for i in range(3):
            p_local[side, 64 * i : 64 * i + 64, :] = dot_nt(values, basis[128 * i : 128 * i + 128, :])
        p_local[side, 192:256, 0:BLOCK] = dot_nt(values, values)
        p_local[side, 192:256, BLOCK:LANES] = jnp.zeros((BLOCK, LANES - BLOCK), F32)
        send_row(lambda o, peer: p_local.at[side, pl.ds(pl.multiple_of(8 * peer, 8), 8)], lambda o: p_rs.at[side, o - 1], p_rs_sem.at[side], send_sem.at[8 + side])

    def sums_ar_send(side):
        wait_bytes(p_rs.at[side], p_rs_sem.at[side])
        total = p_local[side, pl.ds(pl.multiple_of(8 * row, 8), 8), :]
        for o in range(ROWS - 1):
            total = total + p_rs[side, o]
        p_ar[side, col] = total
        send_col(lambda o, peer: p_ar.at[side, col], lambda o: p_ar.at[side, col], p_ar_sem.at[side], send_sem.at[10 + side])

    def sums_ag_send(side):
        wait_bytes(p_ar.at[side, pl.ds(0, COLS - 1)], p_ar_sem.at[side])
        total = p_ar[side, 0]
        for c in range(1, COLS):
            total = total + p_ar[side, c]
        p_all[side, row] = total
        send_row(lambda o, peer: p_all.at[side, row], lambda o: p_all.at[side, row], p_ag_sem.at[side], send_sem.at[12 + side])

    def sums_wait(side):
        wait_bytes(p_all.at[side, pl.ds(0, ROWS - 1)], p_ag_sem.at[side])

    def finish(side, values, basis):
        sums = [jnp.concatenate([p_all[side, 8 * i + t] for t in range(8)], axis=0) for i in range(4)]
        joint = jnp.concatenate(sums[0:3], axis=1)
        gram = sums[3][:, 0:BLOCK] - dot_nt(dot_nn(joint, weights[...]), joint)
        projected = values - dot_nn(joint * (1.0 / N), basis[...])
        eliminated = cholesky_and_inverse(gram * (1.0 / N))
        new_block = dot_nn(eliminated[:, BLOCK:LANES], projected)
        upper = jnp.where(lane16 >= lax.broadcasted_iota(jnp.int32, (BLOCK, LANES), 0), eliminated, 0.0)
        return new_block, upper

    def write_factor(side, upper):
        found_out[128 + 64 * side : 192 + 64 * side, 0:BLOCK] = jnp.transpose(upper)[0:BLOCK, :]

    sums_rs_send(0, image, left_set)
    gram_ar_send(0)
    sums_ar_send(0)
    gram_ag_send(0)
    sums_ag_send(0)
    gram_wait(0)
    sums_wait(0)
    left_new, left_upper = finish(0, image, left_set)
    u_slots[col] = pack(left_new, q_left).astype(BF16)
    send_col(lambda o, peer: u_slots.at[col], lambda o: u_slots.at[col], u_sem, send_sem.at[14])
    gram_rs_send(1)
    found_out[0:64, :] = pltpu.roll(left_new, left_back, 1)
    write_factor(0, left_upper)

    wait_bytes(u_slots.at[pl.ds(0, COLS - 1)], u_sem)
    u_all[...] = joined(lambda k: u_slots[k])

    def multiply_back(y):
        target = lax.rem(plane + y, 4)
        part = lax.dot_general(
            u_all[...], matrix[:, pl.ds(pl.multiple_of(768 * target, 768), 768)], (((1,), (0,)), ((), ())), preferred_element_type=F32
        )
        for half in range(2):
            for k, piece in enumerate(pieces(part[:, 384 * half : 384 * half + 384])):
                pair_send[y, k % 2, 2 * half + k // 2] = piece
        pltpu.make_async_remote_copy(
            src_ref=pair_send.at[y, 1 - core], dst_ref=pair_recv.at[y], send_sem=send_sem.at[17], recv_sem=pair_sem.at[y],
            device_id=(col, sibling), device_id_type=MESH,
        ).start()

    def send_pieces(y):
        wait_bytes(pair_recv.at[y], pair_sem.at[y])
        for x in range(4):
            co_send[y, x] = (pair_send[y, core, x] + pair_recv[y, x]).astype(BF16)

        def send_piece(peer, x):
            pltpu.make_async_remote_copy(
                src_ref=co_send.at[y, x], dst_ref=co_recv.at[y, across], send_sem=send_sem.at[15], recv_sem=co_sem.at[y],
                device_id=(col, peer), device_id_type=MESH,
            ).start()

        to_plane(y, send_piece)

    multiply_back(2)
    multiply_back(1)
    send_pieces(2)
    multiply_back(3)
    send_pieces(1)
    multiply_back(0)
    send_pieces(3)
    send_pieces(0)
    co_recv[0, across] = co_send[0, across]
    gram_ar_send(1)
    coimage = jnp.zeros((48, LANES), F32)
    for y in (0, 1, 3, 2):
        wait_bytes(co_recv.at[y, pl.ds(0, 3 if y == 0 else 4)], co_sem.at[y])
        for x in range(4):
            coimage = coimage + co_recv[y, x].astype(F32)
    coimage = jnp.where(valid_right, unpack(coimage, q_right), 0.0)
    sums_rs_send(1, coimage, right_set)
    sums_ar_send(1)
    gram_ag_send(1)
    sums_ag_send(1)
    gram_wait(1)
    sums_wait(1)
    right_new, right_upper = finish(1, coimage, right_set)
    found_out[64:128, :] = pltpu.roll(right_new, right_back, 1)
    write_factor(1, right_upper)

    wait_bytes(b_slots.at[pl.ds(0, 15)], send_sem.at[0])
    wait_bytes(b_slots.at[pl.ds(0, 16)], send_sem.at[16])
    wait_bytes(image_recv, send_sem.at[7])
    wait_bytes(u_slots.at[pl.ds(0, COLS - 1)], send_sem.at[14])
    for y in range(4):
        wait_bytes(co_recv.at[y, pl.ds(0, 3 if y == 0 else 4)], send_sem.at[15])
        wait_bytes(pair_recv.at[y], send_sem.at[17])
    for side in range(2):
        wait_bytes(g_rs.at[side], send_sem.at[1 + side])
        wait_bytes(g_ar.at[side, pl.ds(0, COLS - 1)], send_sem.at[3 + side])
        wait_bytes(g_all.at[side, pl.ds(0, ROWS - 1)], send_sem.at[5 + side])
        wait_bytes(p_rs.at[side], send_sem.at[8 + side])
        wait_bytes(p_ar.at[side, pl.ds(0, COLS - 1)], send_sem.at[10 + side])
        wait_bytes(p_all.at[side, pl.ds(0, ROWS - 1)], send_sem.at[12 + side])


def shards(matrix, left_basis, right_basis, right_block):
    in_hbm = pl.BlockSpec(memory_space=pltpu.HBM)
    in_vmem = pl.BlockSpec(memory_space=pltpu.VMEM)
    dma = pltpu.SemaphoreType.DMA
    found = pl.pallas_call(
        kernel,
        out_shape=jax.ShapeDtypeStruct((4 * BLOCK, LANES), F32),
        in_specs=[in_hbm] * 4,
        out_specs=in_vmem,
        scratch_shapes=[
            pltpu.VMEM((768, 3072), BF16),
            pltpu.VMEM((WIDTH, PRIOR_ROWS), F32),
            pltpu.VMEM((WIDTH, PRIOR_ROWS), F32),
            pltpu.VMEM((BLOCK, WIDTH), F32),
            pltpu.VMEM((LANES, SET_ROWS), F32),
            pltpu.VMEM((SET_ROWS, LANES), F32),
            pltpu.VMEM((SET_ROWS, LANES), F32),
            pltpu.VMEM((ROWS, 48, LANES), BF16),
            pltpu.VMEM((BLOCK, 768), BF16),
            pltpu.VMEM((BLOCK, 768), F32),
            pltpu.VMEM((COLS, 48, LANES), F32),
            pltpu.VMEM((COLS - 1, 48, LANES), F32),
            pltpu.VMEM((COLS, 48, LANES), BF16),
            pltpu.VMEM((BLOCK, 768), BF16),
            pltpu.VMEM((4, 2, 4, 48, LANES), F32),
            pltpu.VMEM((4, 4, 48, LANES), F32),
            pltpu.VMEM((4, 4, 48, LANES), BF16),
            pltpu.VMEM((4, 4, 48, LANES), BF16),
            pltpu.VMEM((2, 256, LANES), F32),
            pltpu.VMEM((2, ROWS - 1, 8, LANES), F32),
            pltpu.VMEM((2, COLS, 8, LANES), F32),
            pltpu.VMEM((2, ROWS, 8, LANES), F32),
            pltpu.VMEM((2, 768, LANES), F32),
            pltpu.VMEM((2, ROWS - 1, 24, LANES), F32),
            pltpu.VMEM((2, COLS, 24, LANES), F32),
            pltpu.VMEM((2, ROWS, 24, LANES), F32),
            pltpu.VMEM((SET_ROWS, SET_ROWS), F32),
            dma((4,)), dma((18,)), dma((4,)), dma((4,)), dma(()), dma(()), dma((4,)), dma((4,)),
            dma((2,)), dma((2,)), dma((2,)), dma((2,)), dma((2,)), dma((2,)),
        ],
        compiler_params=pltpu.CompilerParams(
            collective_id=0, has_side_effects=True, vmem_limit_bytes=(53 * 1024 + 768) * 1024
        ),
        cost_estimate=pl.CostEstimate(flops=700_000_000, bytes_accessed=8_000_000, transcendentals=0),
    )(matrix, left_basis.T, right_basis.T, right_block)
    factors = found[128:256, 0:BLOCK].reshape(2, BLOCK, BLOCK)
    return found[0:64, 0:WIDTH], found[64:128, 0:WIDTH], factors


def solution(mesh):
    in_specs = (
        P("row", "col"),
        P(None, ("row", "col")),
        P(None, ("col", "row")),
        P(None, ("col", "row")),
    )
    out_specs = (P(None, ("row", "col")), P(None, ("col", "row")), P())
    return jax.shard_map(shards, mesh=mesh, in_specs=in_specs, out_specs=out_specs, check_vma=False)
```

```python
import jax
import jax.numpy as jnp
from jax import lax
from jax.experimental import pallas as pl
from jax.experimental.pallas import tpu as pltpu
from jax.sharding import PartitionSpec as P

N = 24576
BLOCK = 64
PRIOR_ROWS = 320
SET_ROWS = 384
COLS = 8
ROWS = 32
WIDTH = 96
LANES = 128
MESH = pl.DeviceIdType.MESH
F32 = jnp.float32
BF16 = jnp.bfloat16
highest_precision = lax.Precision.HIGHEST


def dot_nn(first, second):
    return lax.dot_general(first, second, (((1,), (0,)), ((), ())), precision=highest_precision, preferred_element_type=F32)


def dot_nt(first, second):
    return lax.dot_general(first, second, (((1,), (1,)), ((), ())), precision=highest_precision, preferred_element_type=F32)


def wait_bytes(ref, sem):
    pltpu.make_async_copy(ref, ref, sem).wait()


def lanes_of(shape):
    return lax.broadcasted_iota(jnp.int32, shape, 1)


def valid_lanes(shape, q):
    return lax.rem(lanes_of(shape) + 32 * q, LANES) < WIDTH


def pack(values, q):
    moved = jnp.concatenate([pltpu.roll(values[48:64, :], 32 * (3 - k), 1) for k in range(3)], axis=0)
    return jnp.where(valid_lanes((48, LANES), q), values[0:48, :], moved)


def unpack(packed, q):
    group = lax.rem(lanes_of((16, LANES)) + 32 * q, LANES)
    back = [pltpu.roll(packed[16 * k : 16 * k + 16, :], 32 * (1 + k), 1) for k in range(3)]
    last = jnp.where(group < 32, back[0], jnp.where(group < 64, back[1], back[2]))
    return jnp.concatenate([packed, last], axis=0)


def cholesky_and_inverse(gram):
    lane = lanes_of((8, LANES))
    sub = lax.broadcasted_iota(jnp.int32, (8, LANES), 0)

    def spread(values):
        return jnp.broadcast_to(values, (8, LANES))

    blocks = []
    for k in range(8):
        unit = jnp.where(lane == sub + (BLOCK + 8 * k), 1.0, 0.0)
        padded = jnp.concatenate([gram[8 * k : 8 * k + 8, :], jnp.zeros((8, BLOCK), F32)], axis=1)
        blocks.append(padded + unit)
    for b in range(8):
        columns = [[spread(blocks[k][:, 8 * b + i : 8 * b + i + 1]) for k in range(b, 8)] for i in range(8)]
        for i in range(8):
            inverse = lax.rsqrt(spread(columns[i][0][i : i + 1, :]))
            lower = [column * inverse for column in columns[i]]
            row = spread(blocks[b][i : i + 1, :]) * inverse
            for m in range(i + 1, 8):
                weight = spread(lower[0][m : m + 1, :])
                columns[m] = [column - below * weight for column, below in zip(columns[m], lower)]
            updated = blocks[b] - lower[0] * row
            blocks[b] = jnp.where(sub > i, updated, jnp.where(sub == i, row, blocks[b]))
            for k in range(b + 1, 8):
                blocks[k] = blocks[k] - lower[k - b] * row
    return jnp.concatenate(blocks, axis=0)


def kernel(
    matrix_hbm, left_hbm, right_hbm, block_hbm,
    found_out,
    matrix, left_in, right_in, block_in,
    turned, left_set, right_set,
    b_slots, b_all, image_sum, image_send, image_recv,
    u_slots, u_all, pair_send, pair_recv, co_send, co_recv,
    p_local, p_rs, p_ar, p_all,
    g_local, g_rs, g_ar, g_all, weights,
    load_sem, send_sem, b_sem, pass_sem, image_sem, u_sem, pair_sem, co_sem,
    p_rs_sem, p_ar_sem, p_ag_sem, g_rs_sem, g_ar_sem, g_ag_sem,
):
    col = lax.axis_index("col")
    row = lax.axis_index("row")
    q_left = lax.rem(col, 4)
    q_right = lax.rem(row, 4)

    def row_peer(o):
        return lax.rem(row + o, ROWS)

    def col_peer(o):
        return lax.rem(col + o, COLS)

    barrier = pltpu.get_barrier_semaphore()

    def greet_row(o, carry):
        pl.semaphore_signal(barrier, inc=1, device_id=(col, row_peer(o)), device_id_type=MESH)
        return carry

    def greet_col(o, carry):
        pl.semaphore_signal(barrier, inc=1, device_id=(col_peer(o), row), device_id_type=MESH)
        return carry

    load_block = pltpu.make_async_copy(block_hbm, block_in, load_sem.at[0])
    load_left = pltpu.make_async_copy(left_hbm, left_in, load_sem.at[1])
    load_right = pltpu.make_async_copy(right_hbm, right_in, load_sem.at[2])
    load_matrix = pltpu.make_async_copy(matrix_hbm, matrix, load_sem.at[3])
    load_block.start()
    lax.fori_loop(1, ROWS, greet_row, 0)
    lax.fori_loop(1, COLS, greet_col, 0)
    load_left.start()
    load_right.start()
    load_matrix.start()

    def send_row(source, target, sem, send):
        def body(k, carry):
            o = lax.rem(k + 15, ROWS - 1) + 1
            peer = row_peer(o)
            pltpu.make_async_remote_copy(
                src_ref=source(o, peer), dst_ref=target(o), send_sem=send, recv_sem=sem,
                device_id=(col, peer), device_id_type=MESH,
            ).start()
            return carry

        lax.fori_loop(0, ROWS - 1, body, 0, unroll=True)

    def send_col(source, target, sem, send):
        def body(k, carry):
            o = lax.rem(k + 3, COLS - 1) + 1
            peer = col_peer(o)
            pltpu.make_async_remote_copy(
                src_ref=source(o, peer), dst_ref=target(o), send_sem=send, recv_sem=sem,
                device_id=(peer, row), device_id_type=MESH,
            ).start()
            return carry

        lax.fori_loop(0, COLS - 1, body, 0, unroll=True)

    right_shift = lax.rem(96 * q_right, LANES)
    right_back = lax.rem(32 * q_right, LANES)
    left_back = lax.rem(32 * q_left, LANES)

    turned[...] = jnp.zeros_like(turned)
    load_block.wait()
    left_set[0:BLOCK, :] = jnp.zeros((BLOCK, LANES), F32)
    left_set[0:BLOCK, 0:WIDTH] = block_in[...]
    turned_block = pltpu.roll(left_set[0:BLOCK, :], right_shift, 1)
    plane, across, core = row // 8, lax.rem(row, 8) // 2, lax.rem(row, 2)
    sibling = row + 1 - 2 * core
    own_slot = 8 * plane + 4 * core + across
    b_slots[own_slot] = pack(turned_block, q_right).astype(BF16)
    pl.semaphore_wait(barrier, ROWS + COLS - 2)

    def chip_peer(y, x):
        return 8 * lax.rem(plane + y, 4) + 2 * x + core

    def to_plane(y, send):
        def near(w, carry):
            x = lax.rem(across + w, 4)
            send(chip_peer(y, x), x)
            return carry

        lax.fori_loop(1 if y == 0 else 0, 4, near, 0, unroll=True)

    for y in (0, 1, 3, 2):

        def send_block(peer, x, y=y):
            pltpu.make_async_remote_copy(
                src_ref=b_slots.at[own_slot], dst_ref=b_slots.at[own_slot], send_sem=send_sem.at[0], recv_sem=b_sem.at[y],
                device_id=(col, peer), device_id_type=MESH,
            ).start()

        to_plane(y, send_block)

    def turn(basis, q, out):
        for k in range(3):
            place = pl.multiple_of(32 * lax.rem(k + 3 * q, 4), 32)
            turned[pl.ds(place, 32), 0:PRIOR_ROWS] = basis[32 * k : 32 * k + 32, :]
        turned[pl.ds(pl.multiple_of(32 * lax.rem(3 + 3 * q, 4), 32), 32), :] = jnp.zeros((32, SET_ROWS), F32)
        for i in range(3):
            out[128 * i : 128 * i + 128, :] = jnp.transpose(turned[:, 128 * i : 128 * i + 128])

    load_left.wait()
    turn(left_in, q_left, left_set)
    load_right.wait()
    turn(right_in, q_right, right_set)
    right_set[PRIOR_ROWS:SET_ROWS, :] = turned_block

    def start_gram(side, basis):
        k = 0
        for i in range(3):
            for j in range(i + 1):
                block = dot_nt(basis[128 * i : 128 * i + 128, :], basis[128 * j : 128 * j + 128, :])
                g_local[side, 128 * k : 128 * k + 128, :] = block
                k += 1

    def gram_rs_send(side):
        send_row(lambda o, peer: g_local.at[side, pl.ds(pl.multiple_of(24 * peer, 8), 24)], lambda o: g_rs.at[side, o - 1], g_rs_sem.at[side], send_sem.at[1 + side])

    def gram_ar_send(side):
        wait_bytes(g_rs.at[side], g_rs_sem.at[side])
        total = g_local[side, pl.ds(pl.multiple_of(24 * row, 8), 24), :]
        for o in range(ROWS - 1):
            total = total + g_rs[side, o]
        g_ar[side, col] = total
        send_col(lambda o, peer: g_ar.at[side, col], lambda o: g_ar.at[side, col], g_ar_sem.at[side], send_sem.at[3 + side])

    def gram_ag_send(side):
        wait_bytes(g_ar.at[side, pl.ds(0, COLS - 1)], g_ar_sem.at[side])
        total = g_ar[side, 0]
        for c in range(1, COLS):
            total = total + g_ar[side, c]
        g_all[side, row] = total
        send_row(lambda o, peer: g_all.at[side, row], lambda o: g_all.at[side, row], g_ag_sem.at[side], send_sem.at[5 + side])

    def gram_wait(side):
        wait_bytes(g_all.at[side, pl.ds(0, ROWS - 1)], g_ag_sem.at[side])
        k = 0
        for i in range(3):
            for j in range(i + 1):
                for t in range(16):
                    at = 128 * k + 8 * t
                    weights[128 * i + 8 * t : 128 * i + 8 * t + 8, 128 * j : 128 * j + 128] = g_all[side, at // 24, at % 24 : at % 24 + 8, :] * (-1.0 / N / N)
                block = weights[128 * i : 128 * i + 128, 128 * j : 128 * j + 128]
                if i == j:
                    same = lanes_of((128, LANES)) == lax.broadcasted_iota(jnp.int32, (128, LANES), 0)
                    weights[128 * i : 128 * i + 128, 128 * j : 128 * j + 128] = block + jnp.where(same, 2.0 / N, 0.0)
                else:
                    weights[128 * j : 128 * j + 128, 128 * i : 128 * i + 128] = jnp.transpose(block)
                k += 1

    start_gram(0, left_set)

    lane16 = lanes_of((BLOCK, LANES))

    def joined(slots):
        chunks = []
        for group in range(2):
            first, second, third, fourth = (unpack(slots(4 * group + k).astype(F32), k) for k in range(4))
            chunks.append(jnp.where(lane16 < 96, first, second).astype(BF16))
            chunks.append(jnp.where(lane16 < 64, second, third).astype(BF16))
            chunks.append(jnp.where(lane16 < 32, third, fourth).astype(BF16))
        return jnp.concatenate(chunks, axis=1)

    def pieces(values):
        first, second, third = (values[:, 128 * k : 128 * k + 128] for k in range(3))
        turned_pieces = (first, jnp.where(lane16 < 64, second, first), jnp.where(lane16 < 64, third, second), third)
        return [pack(piece, k) for k, piece in enumerate(turned_pieces)]

    load_matrix.wait()
    def pass_to_sibling(y):
        wait_bytes(b_slots.at[pl.ds(0, 3 if y == 0 else 4)], b_sem.at[y])
        own = b_slots.at[pl.ds(8 * lax.rem(plane + (4 - y), 4) + 4 * core, 4)]
        pltpu.make_async_remote_copy(
            src_ref=own, dst_ref=own, send_sem=send_sem.at[16], recv_sem=pass_sem.at[y],
            device_id=(col, sibling), device_id_type=MESH,
        ).start()

    def multiply(y):
        wait_bytes(b_slots.at[pl.ds(0, 4)], pass_sem.at[y])
        source = lax.rem(plane + (4 - y), 4)
        b_all[...] = joined(lambda k: b_slots[8 * source + 4 * (k % 2) + k // 2])
        part = lax.dot_general(
            b_all[...], matrix[:, pl.ds(pl.multiple_of(768 * source, 768), 768)], (((1,), (1,)), ((), ())), preferred_element_type=F32
        )
        if y == 0:
            image_sum[...] = part
        else:
            image_sum[...] += part

    pass_to_sibling(0)
    pass_to_sibling(1)
    multiply(0)
    pass_to_sibling(3)
    multiply(1)
    pass_to_sibling(2)
    multiply(3)
    multiply(2)
    for half in range(2):
        for k, piece in enumerate(pieces(image_sum[:, 384 * half : 384 * half + 384])):
            image_send[4 * half + k] = piece
    send_col(lambda o, peer: image_send.at[peer], lambda o: image_recv.at[o - 1], image_sem, send_sem.at[7])
    gram_rs_send(0)
    start_gram(1, right_set)
    wait_bytes(image_recv, image_sem)
    valid_left = valid_lanes((BLOCK, LANES), q_left)
    valid_right = valid_lanes((BLOCK, LANES), q_right)
    image = image_send[col]
    for o in range(COLS - 1):
        image = image + image_recv[o]
    image = jnp.where(valid_left, unpack(image, q_left), 0.0)

    def sums_rs_send(side, values, basis):
        for i in range(3):
            p_local[side, 64 * i : 64 * i + 64, :] = dot_nt(values, basis[128 * i : 128 * i + 128, :])
        p_local[side, 192:256, 0:BLOCK] = dot_nt(values, values)
        p_local[side, 192:256, BLOCK:LANES] = jnp.zeros((BLOCK, LANES - BLOCK), F32)
        send_row(lambda o, peer: p_local.at[side, pl.ds(pl.multiple_of(8 * peer, 8), 8)], lambda o: p_rs.at[side, o - 1], p_rs_sem.at[side], send_sem.at[8 + side])

    def sums_ar_send(side):
        wait_bytes(p_rs.at[side], p_rs_sem.at[side])
        total = p_local[side, pl.ds(pl.multiple_of(8 * row, 8), 8), :]
        for o in range(ROWS - 1):
            total = total + p_rs[side, o]
        p_ar[side, col] = total
        send_col(lambda o, peer: p_ar.at[side, col], lambda o: p_ar.at[side, col], p_ar_sem.at[side], send_sem.at[10 + side])

    def sums_ag_send(side):
        wait_bytes(p_ar.at[side, pl.ds(0, COLS - 1)], p_ar_sem.at[side])
        total = p_ar[side, 0]
        for c in range(1, COLS):
            total = total + p_ar[side, c]
        p_all[side, row] = total
        send_row(lambda o, peer: p_all.at[side, row], lambda o: p_all.at[side, row], p_ag_sem.at[side], send_sem.at[12 + side])

    def sums_wait(side):
        wait_bytes(p_all.at[side, pl.ds(0, ROWS - 1)], p_ag_sem.at[side])

    def finish(side, values, basis):
        sums = [jnp.concatenate([p_all[side, 8 * i + t] for t in range(8)], axis=0) for i in range(4)]
        joint = jnp.concatenate(sums[0:3], axis=1)
        gram = sums[3][:, 0:BLOCK] - dot_nt(dot_nn(joint, weights[...]), joint)
        projected = values - dot_nn(joint * (1.0 / N), basis[...])
        eliminated = cholesky_and_inverse(gram * (1.0 / N))
        new_block = dot_nn(eliminated[:, BLOCK:LANES], projected)
        upper = jnp.where(lane16 >= lax.broadcasted_iota(jnp.int32, (BLOCK, LANES), 0), eliminated, 0.0)
        return new_block, upper

    def write_factor(side, upper):
        found_out[128 + 64 * side : 192 + 64 * side, 0:BLOCK] = jnp.transpose(upper)[0:BLOCK, :]

    sums_rs_send(0, image, left_set)
    gram_ar_send(0)
    sums_ar_send(0)
    gram_ag_send(0)
    sums_ag_send(0)
    gram_wait(0)
    sums_wait(0)
    left_new, left_upper = finish(0, image, left_set)
    u_slots[col] = pack(left_new, q_left).astype(BF16)
    send_col(lambda o, peer: u_slots.at[col], lambda o: u_slots.at[col], u_sem, send_sem.at[14])
    gram_rs_send(1)
    found_out[0:64, :] = pltpu.roll(left_new, left_back, 1)
    write_factor(0, left_upper)

    wait_bytes(u_slots.at[pl.ds(0, COLS - 1)], u_sem)
    u_all[...] = joined(lambda k: u_slots[k])

    def multiply_back(y):
        target = lax.rem(plane + y, 4)
        part = lax.dot_general(
            u_all[...], matrix[:, pl.ds(pl.multiple_of(768 * target, 768), 768)], (((1,), (0,)), ((), ())), preferred_element_type=F32
        )
        for half in range(2):
            for k, piece in enumerate(pieces(part[:, 384 * half : 384 * half + 384])):
                pair_send[y, k % 2, 2 * half + k // 2] = piece
        pltpu.make_async_remote_copy(
            src_ref=pair_send.at[y, 1 - core], dst_ref=pair_recv.at[y], send_sem=send_sem.at[17], recv_sem=pair_sem.at[y],
            device_id=(col, sibling), device_id_type=MESH,
        ).start()

    def send_pieces(y):
        wait_bytes(pair_recv.at[y], pair_sem.at[y])
        for x in range(4):
            co_send[y, x] = (pair_send[y, core, x] + pair_recv[y, x]).astype(BF16)

        def send_piece(peer, x):
            pltpu.make_async_remote_copy(
                src_ref=co_send.at[y, x], dst_ref=co_recv.at[y, across], send_sem=send_sem.at[15], recv_sem=co_sem.at[y],
                device_id=(col, peer), device_id_type=MESH,
            ).start()

        to_plane(y, send_piece)

    multiply_back(2)
    multiply_back(1)
    send_pieces(2)
    multiply_back(3)
    send_pieces(1)
    multiply_back(0)
    send_pieces(3)
    send_pieces(0)
    co_recv[0, across] = co_send[0, across]
    gram_ar_send(1)
    coimage = jnp.zeros((48, LANES), F32)
    for y in (0, 1, 3, 2):
        wait_bytes(co_recv.at[y, pl.ds(0, 3 if y == 0 else 4)], co_sem.at[y])
        for x in range(4):
            coimage = coimage + co_recv[y, x].astype(F32)
    coimage = jnp.where(valid_right, unpack(coimage, q_right), 0.0)
    sums_rs_send(1, coimage, right_set)
    sums_ar_send(1)
    gram_ag_send(1)
    sums_ag_send(1)
    gram_wait(1)
    sums_wait(1)
    right_new, right_upper = finish(1, coimage, right_set)
    found_out[64:128, :] = pltpu.roll(right_new, right_back, 1)
    write_factor(1, right_upper)

    wait_bytes(b_slots.at[pl.ds(0, 15)], send_sem.at[0])
    wait_bytes(b_slots.at[pl.ds(0, 16)], send_sem.at[16])
    wait_bytes(image_recv, send_sem.at[7])
    wait_bytes(u_slots.at[pl.ds(0, COLS - 1)], send_sem.at[14])
    for y in range(4):
        wait_bytes(co_recv.at[y, pl.ds(0, 3 if y == 0 else 4)], send_sem.at[15])
        wait_bytes(pair_recv.at[y], send_sem.at[17])
    for side in range(2):
        wait_bytes(g_rs.at[side], send_sem.at[1 + side])
        wait_bytes(g_ar.at[side, pl.ds(0, COLS - 1)], send_sem.at[3 + side])
        wait_bytes(g_all.at[side, pl.ds(0, ROWS - 1)], send_sem.at[5 + side])
        wait_bytes(p_rs.at[side], send_sem.at[8 + side])
        wait_bytes(p_ar.at[side, pl.ds(0, COLS - 1)], send_sem.at[10 + side])
        wait_bytes(p_all.at[side, pl.ds(0, ROWS - 1)], send_sem.at[12 + side])


def shards(matrix, left_basis, right_basis, right_block):
    in_hbm = pl.BlockSpec(memory_space=pltpu.HBM)
    in_vmem = pl.BlockSpec(memory_space=pltpu.VMEM)
    dma = pltpu.SemaphoreType.DMA
    found = pl.pallas_call(
        kernel,
        out_shape=jax.ShapeDtypeStruct((4 * BLOCK, LANES), F32),
        in_specs=[in_hbm] * 4,
        out_specs=in_vmem,
        scratch_shapes=[
            pltpu.VMEM((768, 3072), BF16),
            pltpu.VMEM((WIDTH, PRIOR_ROWS), F32),
            pltpu.VMEM((WIDTH, PRIOR_ROWS), F32),
            pltpu.VMEM((BLOCK, WIDTH), F32),
            pltpu.VMEM((LANES, SET_ROWS), F32),
            pltpu.VMEM((SET_ROWS, LANES), F32),
            pltpu.VMEM((SET_ROWS, LANES), F32),
            pltpu.VMEM((ROWS, 48, LANES), BF16),
            pltpu.VMEM((BLOCK, 768), BF16),
            pltpu.VMEM((BLOCK, 768), F32),
            pltpu.VMEM((COLS, 48, LANES), F32),
            pltpu.VMEM((COLS - 1, 48, LANES), F32),
            pltpu.VMEM((COLS, 48, LANES), BF16),
            pltpu.VMEM((BLOCK, 768), BF16),
            pltpu.VMEM((4, 2, 4, 48, LANES), F32),
            pltpu.VMEM((4, 4, 48, LANES), F32),
            pltpu.VMEM((4, 4, 48, LANES), BF16),
            pltpu.VMEM((4, 4, 48, LANES), BF16),
            pltpu.VMEM((2, 256, LANES), F32),
            pltpu.VMEM((2, ROWS - 1, 8, LANES), F32),
            pltpu.VMEM((2, COLS, 8, LANES), F32),
            pltpu.VMEM((2, ROWS, 8, LANES), F32),
            pltpu.VMEM((2, 768, LANES), F32),
            pltpu.VMEM((2, ROWS - 1, 24, LANES), F32),
            pltpu.VMEM((2, COLS, 24, LANES), F32),
            pltpu.VMEM((2, ROWS, 24, LANES), F32),
            pltpu.VMEM((SET_ROWS, SET_ROWS), F32),
            dma((4,)), dma((18,)), dma((4,)), dma((4,)), dma(()), dma(()), dma((4,)), dma((4,)),
            dma((2,)), dma((2,)), dma((2,)), dma((2,)), dma((2,)), dma((2,)),
        ],
        compiler_params=pltpu.CompilerParams(
            collective_id=0, has_side_effects=True, vmem_limit_bytes=(53 * 1024 + 768) * 1024
        ),
        cost_estimate=pl.CostEstimate(flops=700_000_000, bytes_accessed=8_000_000, transcendentals=0),
    )(matrix, left_basis.T, right_basis.T, right_block)
    factors = found[128:256, 0:BLOCK].reshape(2, BLOCK, BLOCK)
    return found[0:64, 0:WIDTH], found[64:128, 0:WIDTH], factors


def solution(mesh):
    in_specs = (
        P("row", "col"),
        P(None, ("row", "col")),
        P(None, ("col", "row")),
        P(None, ("col", "row")),
    )
    out_specs = (P(None, ("row", "col")), P(None, ("col", "row")), P())
    return jax.shard_map(shards, mesh=mesh, in_specs=in_specs, out_specs=out_specs, check_vma=False)
```
